128 devices in a mesh: dp: 16 (over x_hi, y, core), seq: 8 (over z, x_lo).
Axes of the slice: x: 4 (x_hi: 2, x_lo: 2; x = x_hi * 2 + x_lo), y: 4, z: 4, core: 2. Of those that a mesh axis runs over, the one named last changes fastest.
Arguments:
- bases: int32 [16, 8192], P('dp', 'seq'), may hold values from 0 to 3
- upsampled: bfloat16 [16, 8192, 768], P('dp', 'seq'), may hold values from -6 to 6
- base_table: bfloat16 [4, 768], replicated, may hold values from -4 to 4
- filter_weight: bfloat16 [5, 768, 768], replicated, may hold values from -0.09375 to 0.09375
- filter_bias: float32 [768], replicated, may hold values from -3 to 3
- norm_gain: float32 [768], replicated, may hold values from 0.5 to 1.5
- cotangent: bfloat16 [16, 8192, 768], P('dp', 'seq'), may hold values from -6 to 6
Outputs:
- block_out: bfloat16 [16, 8192, 768], P('dp', 'seq')
- grad_input: bfloat16 [16, 8192, 768], P('dp', 'seq')
- grad_weight: float32 [5, 768, 768], P(None, ('dp', 'seq'))
- grad_bias: float32 [768], P(('dp', 'seq'))
- grad_gain: float32 [768], P(('dp', 'seq'))
The draws below stay inside these ranges and needn't reach their ends.
All inputs are finite; a program needn't handle non-finite values.
Results may differ from the reference program's by a relative error of at most 0.0085.
Values may be sent and summed in bfloat16 or wider, within the bound.
A program may use at most 128 MiB of HBM per device.

```python
import jax
import jax.numpy as jnp
from jax import lax

C = 768
TAP_COUNT = 5
SIDE_TAPS = 2
DILATION_STEP = 4
WINDOW_LENGTH = 8192
NWIN = 16


def with_ends(array, rng, least, largest):
    place = [jax.random.randint(jax.random.fold_in(rng, axis), (), 0, length) for axis, length in enumerate(array.shape)]
    main_axis = array.shape.index(max(array.shape))
    beside = place[:main_axis] + [(place[main_axis] + 1) % array.shape[main_axis]] + place[main_axis + 1:]
    return array.at[tuple(place)].set(least).at[tuple(beside)].set(largest)


def raised(entries, own_key, source, target, shards_of, factor):
    def block_of(position):
        return (jnp.arange(entries.shape[position]) // (entries.shape[position] // shards_of)).reshape((-1,) + (1,) * (entries.ndim - 1 - position))

    near = jax.random.permutation(own_key, shards_of)[block_of(target)]
    far = (block_of(target) + shards_of // 2) % shards_of
    return jnp.where((block_of(source) == near) | (block_of(source) == far), factor * entries, entries)


def block_levels(own_key, shape, cuts, least, top_value):
    def one(dim, shards_of):
        draws = jax.random.uniform(jax.random.fold_in(jax.random.fold_in(own_key, 6), dim), (shards_of,), jnp.float32, least / len(cuts), top_value / len(cuts))
        return jnp.repeat(jnp.exp(draws), shape[dim] // shards_of).reshape((-1,) + (1,) * (len(shape) - dim - 1))

    factor_of = one(*cuts[0])
    for cut in cuts[1:]:
        factor_of = factor_of * one(*cut)
    return factor_of


def gaussian(rng, shape, spread, bound, pieces=(), kind=jnp.bfloat16):
    level = block_levels(rng, shape, pieces, -0.22, 0.18) if pieces else 1.0
    array = jax.random.normal(rng, shape, jnp.float32) * spread * level
    return jnp.minimum(jnp.maximum(array, -bound), bound).astype(kind)


def bell_draw_with(stream_key, shape, spread, bound, shards, heavy, kind=jnp.bfloat16):
    array = spread * jax.random.normal(stream_key, shape, jnp.float32)
    if shards:
        array = array * block_levels(stream_key, shape, shards, -0.22, 0.18)
    return jnp.clip(raised(array, jax.random.fold_in(stream_key, 3), *heavy), -bound, bound).astype(kind)


def setup_inputs(seed: int = 0) -> dict:
    key_of = jax.random.split(jax.random.key(seed), 8)
    return {
        "bases": with_ends(jax.random.randint(key_of[0], (NWIN, WINDOW_LENGTH), 0, 4), jax.random.fold_in(key_of[0], 1), 0, 3).astype(jnp.int32),
        "upsampled": gaussian(key_of[1], (NWIN, WINDOW_LENGTH, C), 1.0, 6.0, ((0, 16), (1, 8))),
        "base_table": gaussian(key_of[2], (4, C), 0.7, 4.0),
        "filter_weight": gaussian(key_of[3], (TAP_COUNT, C, C), (TAP_COUNT * C) ** -0.5, 0.09375),
        "filter_bias": gaussian(key_of[4], (C,), 0.5, 3.0, (), jnp.float32),
        "norm_gain": jnp.clip(1.0 + 0.1 * jax.random.normal(key_of[5], (C,), jnp.float32), 0.5, 1.5),
        "cotangent": bell_draw_with(key_of[6], (NWIN, WINDOW_LENGTH, C), 1.0, 6.0, ((0, 16), (1, 8)), (1, 2, 8, 2.0)),
    }


def window_pass(bases_w, up_w, cot_w, base_table, filter_weight, filter_bias, norm_gain):
    channel_width = SIDE_TAPS * DILATION_STEP
    onehot = (bases_w[:, None] == jnp.arange(4, dtype=jnp.int32)[None, :]).astype(jnp.bfloat16)
    x = up_w.astype(jnp.float32) + jnp.dot(onehot, base_table, preferred_element_type=jnp.float32)
    rms = jnp.sqrt(lax.optimization_barrier(jnp.mean(x * x, axis=-1, keepdims=True)) + 1e-06)
    normed = x / rms
    h = (normed * norm_gain).astype(jnp.bfloat16)
    padded_input = jnp.pad(h, ((channel_width, channel_width), (0, 0)))
    preactivation = filter_bias[None, :] + sum((jnp.dot(padded_input[tap_index * DILATION_STEP:tap_index * DILATION_STEP + WINDOW_LENGTH], filter_weight[tap_index], preferred_element_type=jnp.float32) for tap_index in range(TAP_COUNT)))
    act, pull = jax.vjp(jax.nn.gelu, preactivation)
    block_out = (x + act).astype(jnp.bfloat16)
    output_gradient = pull(cot_w.astype(jnp.float32))[0].astype(jnp.bfloat16)
    padded_gradient = jnp.pad(output_gradient, ((channel_width, channel_width), (0, 0)))
    weight_gradient = jnp.stack([jnp.dot(padded_input[tap_index * DILATION_STEP:tap_index * DILATION_STEP + WINDOW_LENGTH].T, output_gradient, preferred_element_type=jnp.float32) for tap_index in range(TAP_COUNT)])
    dbias = lax.optimization_barrier(jnp.sum(output_gradient.astype(jnp.float32), axis=0))
    hidden_gradient = sum((jnp.dot(padded_gradient[(2 * SIDE_TAPS - tap_index) * DILATION_STEP:(2 * SIDE_TAPS - tap_index) * DILATION_STEP + WINDOW_LENGTH], filter_weight[tap_index].T, preferred_element_type=jnp.float32) for tap_index in range(TAP_COUNT)))
    dgain = lax.optimization_barrier(jnp.sum(hidden_gradient * normed, axis=0))
    dn = hidden_gradient * norm_gain
    grad_in = cot_w.astype(jnp.float32) + (dn - normed * lax.optimization_barrier(jnp.mean(dn * normed, axis=-1, keepdims=True))) / rms
    return (block_out, grad_in.astype(jnp.bfloat16), weight_gradient, dbias, dgain)

def reference(bases, upsampled, base_table, filter_weight, filter_bias, norm_gain, cotangent):

    def step(carry, items):
        out_w, gin_w, weight_gradient, dbias, dgain = window_pass(items[0], items[1], items[2], base_table, filter_weight, filter_bias, norm_gain)
        return ((carry[0] + weight_gradient, carry[1] + dbias, carry[2] + dgain), (out_w, gin_w))
    start = (jnp.zeros((TAP_COUNT, C, C), jnp.float32), jnp.zeros((C,), jnp.float32), jnp.zeros((C,), jnp.float32))
    sums, outs = lax.scan(step, start, (bases, upsampled, cotangent))
    return (outs[0], outs[1], sums[0], sums[1], sums[2])
```

```python
import jax
import jax.numpy as jnp
import numpy as np
from jax import lax
from jax.experimental import pallas as pl
from jax.experimental.pallas import tpu as pltpu
from jax.sharding import PartitionSpec as P

BF, F32 = jnp.bfloat16, jnp.float32
C, TAPS, STEP = 768, 5, 4
ROWS, HALO = 1024, 16
EXT = ROWS + 2 * HALO
WIDE = 256
GROUPS = C // WIDE
HALF = C // 2
NT = (((1,), (1,)), ((), ()))
TN = (((0,), (0,)), ((), ()))

ORDERS = ((0, 1, 2), (1, 0, 2), (2, 0, 1))
PIECES = [
    (group, kind, [k for k in range(TAPS) if (k + group) % 3 == kind])
    for group in range(GROUPS)
    for kind in ((0, 1, 2) if group < 2 else (0, 2, 1))
]
BIAS_PIECE = next(q for q, (group, kind, taps) in enumerate(PIECES) if group == 2 and len(taps) == 1)


def width(q):
    return WIDE * len(PIECES[q][2]) + (128 if q == BIAS_PIECE else 0)


def permutations():
    perm = np.zeros((C, C), np.float32)
    perm_z = np.zeros((HALF, HALF), np.float32)
    for core in range(2):
        for x in range(4):
            for y in range(4):
                for z in range(4):
                    for j in range(6):
                        row = ((x * 4 + y) * 4 + z) * 6 + j
                        source = (x // 2) * 384 + y * 96 + core * 48 + z * 12 + (x % 2) * 6 + j
                        perm[core * HALF + row, source] = 1
                        perm_z[((z * 4 + x) * 4 + y) * 6 + j, row] = 1
    return perm, perm_z


def here():
    dp, seq = lax.axis_index("dp"), lax.axis_index("seq")
    x = 2 * lax.div(dp, 8) + lax.rem(seq, 2)
    return [x, lax.rem(lax.div(dp, 2), 4), lax.div(seq, 2)], lax.rem(dp, 2), dp, seq


def place(pos, core):
    x, y, z = pos
    return (lax.div(x, 2) * 8 + y * 2 + core, z * 2 + lax.rem(x, 2))


def moved(pos, axis, delta):
    other = list(pos)
    other[axis] = lax.rem(pos[axis] + delta, 4)
    return other


def kernel(*refs):
    names = iter(refs)

    def take(n):
        return [next(names) for _ in range(n)]

    bases, up, table, weight, bias, gain, cot, perm, perm_z = take(9)
    out, gin, gw, gbias, ggain = take(5)
    (bases_e, up_e, cot_e, w_v, perm_v, permz_v, tab, xs, rin, hb, h5, hT, hsend, pre) = take(14)
    gbuf, gpar, g5, g5p, bsum, ob, gi, dhs, gws = take(9)
    bufs = [take(6) for _ in PIECES]
    local_sem, send_sem, recv_sem = take(3)

    pos, core, dp, seq = here()
    partner = place(pos, 1 - core)
    left, right = (dp, lax.rem(seq + 7, 8)), (dp, lax.rem(seq + 1, 8))
    remote_count, local_count, started = [0], [0], []

    def remote(src, dst, device):
        n = remote_count[0]
        remote_count[0] += 1
        copy = pltpu.make_async_remote_copy(
            src_ref=src, dst_ref=dst, send_sem=send_sem.at[n], recv_sem=recv_sem.at[n],
            device_id=device, device_id_type=MESH,
        )
        copy.start()
        started.append(copy)
        return copy

    def local(src, dst):
        n = local_count[0]
        local_count[0] += 1
        copy = pltpu.make_async_copy(src, dst, local_sem.at[n])
        copy.start()
        return copy

    in_bases = local(bases, bases_e.at[:, pl.ds(128, ROWS)])
    in_up = local(up, up_e.at[pl.ds(HALO, ROWS)])
    in_perm = [
        local(perm.at[pl.ds(pl.multiple_of(c * HALF, HALF), HALF)], perm_v.at[pl.ds(half * HALF, HALF)])
        for half, c in enumerate((core, 1 - core))
    ]
    in_w = [local(weight.at[:, pl.ds(p * WIDE, WIDE)], w_v.at[:, pl.ds(p * WIDE, WIDE)]) for p in range(GROUPS)]
    in_cot = local(cot, cot_e.at[pl.ds(HALO, ROWS)])
    in_permz = local(perm_z, permz_v)

    barrier = pltpu.get_barrier_semaphore()
    partners = [partner, left, right]
    partners += [place(moved(pos, axis, delta), core) for axis in range(3) for delta in (1, 2, 3)]
    for device in partners:
        pl.semaphore_signal(barrier, inc=1, device_id=device, device_id_type=MESH)
    pl.semaphore_wait(barrier, len(partners))

    halos = [
        remote(bases.at[:, pl.ds(ROWS - 128, 128)], bases_e.at[:, pl.ds(0, 128)], right),
        remote(bases.at[:, pl.ds(0, 128)], bases_e.at[:, pl.ds(128 + ROWS, 128)], left),
    ]
    for source, target in ((up, up_e), (cot, cot_e)):
        halos += [
            remote(source.at[pl.ds(ROWS - HALO, HALO)], target.at[pl.ds(0, HALO)], right),
            remote(source.at[pl.ds(0, HALO)], target.at[pl.ds(HALO + ROWS, HALO)], left),
        ]

    tab[...] = jnp.zeros(tab.shape, F32)
    tab[0:4, :] = table[...].astype(F32)
    code = lax.broadcasted_iota(jnp.int32, (8, 128), 0)

    def embedded(block):
        onehot = (code == bases_e[:, pl.ds(pl.multiple_of(block * 128, 128), 128)]).astype(F32)
        return lax.dot_general(onehot, tab[...], TN, preferred_element_type=F32)

    def normed_of(x):
        r = lax.rsqrt(jnp.mean(x * x, axis=-1, keepdims=True) + 1e-06)
        return r, (x * r * gain[...])

    in_bases.wait()
    in_up.wait()

    def norm_block(b, carry):
        e = embedded(b + 1)
        for s in range(4):
            row = pl.multiple_of(b * 128 + s * 32, 32)
            x = up_e[pl.ds(row + HALO, 32), :].astype(F32) + e[s * 32 : s * 32 + 32]
            r, h = normed_of(x)
            xs[pl.ds(row, 32), :] = x
            rin[pl.ds(row, 32), :] = jnp.broadcast_to(r, (32, 128))
            hb[pl.ds(row + 2 * HALO, 32), :] = h.astype(BF)
        return carry

    lax.fori_loop(0, ROWS // 128, norm_block, 0)
    for copy in halos:
        copy.wait_recv()
    hb[0:HALO, :] = jnp.zeros((HALO, C), BF)
    hb[HALO + EXT : 2 * HALO + EXT, :] = jnp.zeros((HALO, C), BF)
    inside = (seq > 0, seq < 7)
    for side, (block, skip) in enumerate(((0, 128 - HALO), (1 + ROWS // 128, 0))):
        start = side * (HALO + ROWS)
        x = up_e[start : start + HALO, :].astype(F32) + embedded(block)[skip : skip + HALO]
        h = jnp.where(inside[side], normed_of(x)[1], 0.0)
        hb[start + HALO : start + 2 * HALO, :] = h.astype(BF)

    for copy in in_perm:
        copy.wait()
    h_own = hb[2 * HALO : 2 * HALO + ROWS, :]
    hsend[...] = lax.dot_general(perm_v[HALF:, :], h_own, NT, preferred_element_type=F32).astype(BF)
    h_copy = remote(hsend, hT.at[:, pl.ds(ROWS, ROWS)], partner)
    hT[:, 0:ROWS] = lax.dot_general(perm_v[0:HALF, :], h_own, NT, preferred_element_type=F32).astype(BF)

    def shift_h(j, carry):
        row = pl.multiple_of(j * 96, 32)
        for p in range(GROUPS):
            v = hb[pl.ds(row, 128), p * WIDE : (p + 1) * WIDE].astype(F32)
            for k in range(TAPS):
                h5[pl.ds(row, 96), k * C + p * WIDE : k * C + (p + 1) * WIDE] = v[8 + STEP * k : 104 + STEP * k].astype(BF)
        return carry

    lax.fori_loop(0, EXT // 96, shift_h, 0)
    bsum[...] = jnp.zeros(bsum.shape, F32)
    in_permz.wait()
    in_cot.wait()
    c0 = np.float32(np.sqrt(2 / np.pi))
    outgoing, g_copies = [], []

    def gelu_pair(z):
        square = z * z
        t = jnp.tanh(c0 * z * (1 + 0.044715 * square))
        cdf = 0.5 + 0.5 * t
        slope = cdf + (0.5 * c0) * z * (1 - t * t) * (1 + 0.134145 * square)
        return z * cdf, slope

    def forward(p):
        cols = slice(p * WIDE, (p + 1) * WIDE)
        in_w[p].wait()
        pre[...] = jnp.dot(h5[...], w_v[:, cols], preferred_element_type=F32)

        def tile(i, carry):
            row = pl.multiple_of(i * 64, 64)
            act, slope = gelu_pair(pre[pl.ds(row + HALO, 64), :] + bias[:, cols])
            ob[pl.ds(row, 64), cols] = (xs[pl.ds(row, 64), cols] + act).astype(BF)
            gbuf[p, pl.ds(row + HALO, 64), :] = (cot_e[pl.ds(row + HALO, 64), cols].astype(F32) * slope).astype(BF)
            return carry

        lax.fori_loop(0, ROWS // 64, tile, 0)
        for side in range(2):
            rows = slice(side * (HALO + ROWS), side * (HALO + ROWS) + HALO)
            _, slope = gelu_pair(pre[rows, :] + bias[:, cols])
            g = jnp.where(inside[side], cot_e[rows, cols].astype(F32) * slope, 0.0)
            gbuf[p, rows, :] = g.astype(BF)
        g_copies.append(remote(gbuf.at[p], gpar.at[p], partner))
        outgoing.append(local(ob.at[:, pl.ds(p * WIDE, WIDE)], out.at[:, pl.ds(p * WIDE, WIDE)]))

    def shift_g(source, p, target, column):
        def tile(j, total):
            row = pl.multiple_of(j * 128, 128)
            v = source[p, pl.ds(row, 160), :].astype(F32)
            for k in range(TAPS):
                col = column(k)
                target[pl.ds(row, 128), col : col + WIDE] = v[24 - STEP * k : 152 - STEP * k].astype(BF)
            return total + jnp.sum(v[16:144].reshape(16, 8, WIDE), axis=0)

        cols = slice(p * WIDE, (p + 1) * WIDE)
        bsum[:, cols] += lax.fori_loop(0, ROWS // 128, tile, jnp.zeros((8, WIDE), F32))

    hops = {}

    def send(q, stage):
        axis = ORDERS[PIECES[q][1]][stage]
        source, target = bufs[q][2 * stage], bufs[q][2 * stage + 1]
        hops[q, stage] = [
            remote(source.at[moved(pos, axis, delta)[axis]], target.at[delta - 1], place(moved(pos, axis, delta), core))
            for delta in (1, 2, 3)
        ]

    def store_first(q, r, col, n):
        kind, target = PIECES[q][1], bufs[q][0]
        if kind == 2:
            r = jnp.dot(permz_v[...], r.astype(BF), preferred_element_type=F32)
        for d in range(4):
            if kind == 1:
                block = jnp.concatenate([r[e * 96 + d * 24 : e * 96 + d * 24 + 24] for e in range(4)], axis=0)
            else:
                block = r[d * 96 : d * 96 + 96]
            target[d, :, col : col + n] = block.astype(BF)

    def weight_piece(q):
        group, _, taps = PIECES[q]
        for n, k in enumerate(taps):
            a = jnp.dot(hT[:, 0:ROWS], g5[:, k * C + group * WIDE : k * C + (group + 1) * WIDE], preferred_element_type=F32)
            b = jnp.dot(hT[:, ROWS:], g5p[:, k * WIDE : (k + 1) * WIDE], preferred_element_type=F32)
            store_first(q, a + b, n * WIDE, WIDE)
        if q == BIAS_PIECE:
            total = jnp.sum(bsum[...], axis=0, keepdims=True)
            total = jnp.broadcast_to(total, (128, C)).astype(BF)
            r = lax.dot_general(perm_v[0:HALF, :], total, NT, preferred_element_type=F32)
            store_first(q, r, WIDE, 128)
        send(q, 0)

    def weight_group(p):
        shift_g(gbuf, p, g5, lambda k: k * C + p * WIDE)
        g_copies[p].wait_recv()
        shift_g(gpar, p, g5p, lambda k: k * WIDE)
        for q, piece in enumerate(PIECES):
            if piece[0] == p:
                weight_piece(q)

    def arrived(q, stage, col, n):
        axis = ORDERS[PIECES[q][1]][stage]
        source, target = bufs[q][2 * stage], bufs[q][2 * stage + 1]
        total = source[pos[axis], :, col : col + n].astype(F32)
        for d in range(3):
            total = total + target[d, :, col : col + n].astype(F32)
        return total

    spread_row = lax.broadcasted_iota(jnp.int32, (64, 32), 0)
    spread_col = lax.broadcasted_iota(jnp.int32, (64, 32), 1)
    within = spread_row & 15
    spread = ((within < 6) & (spread_col == 6 * (spread_row >> 4) + within)).astype(F32).astype(BF)

    def finish(q, stage):
        for copy in hops[q, stage]:
            copy.wait_recv()
        group, _, taps = PIECES[q]
        for col in range(0, width(q), WIDE):
            n = min(WIDE, width(q) - col)
            total = arrived(q, stage, col, n)
            if stage == 0:
                for d in range(4):
                    block = jnp.concatenate([total[24 * d : 24 * d + 24], jnp.zeros((8, n), F32)], axis=0)
                    bufs[q][2][d, :, col : col + n] = block.astype(BF)
            elif stage == 1:
                r = jnp.dot(spread, total.astype(BF), preferred_element_type=F32).astype(BF)
                for d in range(4):
                    bufs[q][4][d, :, col : col + n] = r[16 * d : 16 * d + 16]
            elif n == WIDE:
                gws[taps[col // WIDE], :, group * WIDE : (group + 1) * WIDE] = total[0:8]
            else:
                gws[TAPS, :, 0:n] = total[0:8]
        if stage < 2:
            send(q, stage + 1)

    def finish_group(p, stage):
        for q, piece in enumerate(PIECES):
            if piece[0] == p:
                finish(q, stage)

    half = ROWS // 2

    def backward(t):
        base = t * half
        dhs[...] = sum(
            lax.dot_general(g5[base : base + half, k * C : (k + 1) * C], w_v[k * C : (k + 1) * C, :], NT, preferred_element_type=F32)
            for k in range(TAPS)
        )

        def tile(i, carry):
            row = pl.multiple_of(i * 32, 32)
            whole = pl.multiple_of(base + i * 32, 32)
            r = rin[pl.ds(whole, 32), 0:1]
            normed = xs[pl.ds(whole, 32), :] * r
            dn = dhs[pl.ds(row, 32), :] * gain[...]
            mean = jnp.mean(dn * normed, axis=-1, keepdims=True)
            g = cot_e[pl.ds(whole + HALO, 32), :].astype(F32) + (dn - normed * mean) * r
            gi[pl.ds(whole, 32), :] = g.astype(BF)
            return carry

        lax.fori_loop(0, half // 32, tile, 0)
        outgoing.append(local(gi.at[pl.ds(base, half)], gin.at[pl.ds(base, half)]))

    forward(0)
    forward(1)
    h_copy.wait_recv()
    weight_group(0)
    forward(2)
    finish_group(0, 0)
    weight_group(1)
    finish_group(0, 1)
    finish_group(1, 0)
    weight_group(2)
    finish_group(0, 2)
    finish_group(1, 1)
    backward(0)
    finish_group(2, 0)
    finish_group(1, 2)
    backward(1)
    finish_group(2, 1)
    finish_group(2, 2)

    gw[...] = gws[0:TAPS, 0:6, :]
    mine = (dp * 8 + seq) * 6
    base = jnp.minimum(lax.div(mine, 16) * 16, C - 32)
    pick_row = lax.broadcasted_iota(jnp.int32, (8, 32), 0)
    pick_col = lax.broadcasted_iota(jnp.int32, (8, 32), 1)
    pick = (pick_col == pick_row + (mine - base)).astype(F32).astype(BF)
    total = jnp.zeros((8, C), F32)
    for k in range(TAPS):
        rows = w_v[pl.ds(pl.multiple_of(k * C + base, 16), 32), :]
        total = total + jnp.dot(pick, rows, preferred_element_type=F32) * gws[k]
    lane = lax.broadcasted_iota(jnp.int32, (8, C), 1)
    row = lax.broadcasted_iota(jnp.int32, (8, C), 0)
    own_gain = jnp.sum(jnp.where(lane == row + mine, gain[...], 0.0), axis=-1, keepdims=True)
    column = jnp.sum(total, axis=-1, keepdims=True) / own_gain
    diagonal = (lane == row)[:, 0:128] & (row < 6)[:, 0:128]
    ggain[...] = jnp.sum(jnp.where(diagonal, column, 0.0), axis=0, keepdims=True)[:, 0:6]
    gbias[...] = jnp.sum(jnp.where(diagonal, gws[TAPS, :, 0:128], 0.0), axis=0, keepdims=True)[:, 0:6]

    for copy in outgoing:
        copy.wait()
    for copy in started:
        copy.wait_send()


MESH = pl.DeviceIdType.MESH


def body(bases, upsampled, base_table, filter_weight, filter_bias, norm_gain, cotangent):
    perm, perm_z = permutations()
    vmem, hbm = pl.BlockSpec(memory_space=pltpu.VMEM), pl.BlockSpec(memory_space=pl.ANY)
    scratch = [
        pltpu.VMEM((1, ROWS + 256), jnp.int32),
        pltpu.VMEM((EXT, C), BF),
        pltpu.VMEM((EXT, C), BF),
        pltpu.VMEM((TAPS * C, C), BF),
        pltpu.VMEM((C, C), BF),
        pltpu.VMEM((HALF, HALF), BF),
        pltpu.VMEM((8, C), F32),
        pltpu.VMEM((ROWS, C), F32),
        pltpu.VMEM((ROWS, 128), F32),
        pltpu.VMEM((EXT + 2 * HALO, C), BF),
        pltpu.VMEM((EXT, TAPS * C), BF),
        pltpu.VMEM((HALF, 2 * ROWS), BF),
        pltpu.VMEM((HALF, ROWS), BF),
        pltpu.VMEM((EXT, WIDE), F32),
        pltpu.VMEM((GROUPS, EXT, WIDE), BF),
        pltpu.VMEM((GROUPS, EXT, WIDE), BF),
        pltpu.VMEM((ROWS, TAPS * C), BF),
        pltpu.VMEM((ROWS, TAPS * WIDE), BF),
        pltpu.VMEM((8, C), F32),
        pltpu.VMEM((ROWS, C), BF),
        pltpu.VMEM((ROWS, C), BF),
        pltpu.VMEM((ROWS // 2, C), F32),
        pltpu.VMEM((TAPS + 1, 8, C), F32),
    ]
    for q in range(len(PIECES)):
        for rows in (96, 32, 16):
            scratch += [pltpu.VMEM((4, rows, width(q)), BF), pltpu.VMEM((3, rows, width(q)), BF)]
    remotes = 6 + 1 + GROUPS + 9 * len(PIECES)
    scratch += [
        pltpu.SemaphoreType.DMA((16,)),
        pltpu.SemaphoreType.DMA((remotes,)),
        pltpu.SemaphoreType.DMA((remotes,)),
    ]
    out, gin, gw, gbias, ggain = pl.pallas_call(
        kernel,
        out_shape=[
            jax.ShapeDtypeStruct((ROWS, C), BF),
            jax.ShapeDtypeStruct((ROWS, C), BF),
            jax.ShapeDtypeStruct((TAPS, 6, C), F32),
            jax.ShapeDtypeStruct((1, 6), F32),
            jax.ShapeDtypeStruct((1, 6), F32),
        ],
        in_specs=[hbm, hbm, vmem, hbm, vmem, vmem, hbm, hbm, hbm],
        out_specs=[hbm, hbm, vmem, vmem, vmem],
        scratch_shapes=scratch,
        compiler_params=pltpu.CompilerParams(collective_id=0, has_side_effects=True, vmem_limit_bytes=62 * 2**20),
        name="block",
    )(
        bases,
        upsampled[0],
        base_table,
        filter_weight.reshape(TAPS * C, C),
        filter_bias[None],
        norm_gain[None],
        cotangent[0],
        jnp.asarray(perm, BF),
        jnp.asarray(perm_z, BF),
    )
    return out[None], gin[None], gw, gbias[0], ggain[0]


def solution(mesh):
    placed = (P("dp", "seq"), P("dp", "seq", None), P(), P(), P(), P(), P("dp", "seq", None))
    return jax.shard_map(
        body,
        mesh=mesh,
        in_specs=placed,
        out_specs=(
            P("dp", "seq", None),
            P("dp", "seq", None),
            P(None, ("dp", "seq"), None),
            P(("dp", "seq")),
            P(("dp", "seq")),
        ),
        check_vma=False,
    )
```

```python
import jax
import jax.numpy as jnp
import numpy as np
from jax import lax
from jax.experimental import pallas as pl
from jax.experimental.pallas import tpu as pltpu
from jax.sharding import PartitionSpec as P

BF, F32 = jnp.bfloat16, jnp.float32
C, TAPS, STEP = 768, 5, 4
ROWS, HALO = 1024, 16
EXT = ROWS + 2 * HALO
WIDE = 256
GROUPS = C // WIDE
HALF = C // 2
NT = (((1,), (1,)), ((), ()))
TN = (((0,), (0,)), ((), ()))

TAP_OF = [3 * slot % TAPS for slot in range(TAPS)]
SLOTS = ((0, 2), (2, 2), (4, 1))
STAGES = 3
TILE = 256
BLOCK_ROWS = (96, 32, 16)


def here():
    dp, seq = lax.axis_index("dp"), lax.axis_index("seq")
    x = 2 * lax.div(dp, 8) + lax.rem(seq, 2)
    return [x, lax.rem(lax.div(dp, 2), 4), lax.div(seq, 2)], lax.rem(dp, 2), dp, seq


def place(pos, core):
    x, y, z = pos
    return (lax.div(x, 2) * 8 + y * 2 + core, z * 2 + lax.rem(x, 2))


def moved(pos, axis, delta):
    other = list(pos)
    other[axis] = lax.rem(pos[axis] + delta, 4)
    return other


def times(value, step):
    return pl.multiple_of(value * step, step)


def kernel(*refs):
    names = iter(refs)

    def take(n):
        return [next(names) for _ in range(n)]

    bases, up, table, weight, bias_in, gain_in, cot = take(7)
    ob, gi, gw, small = take(4)
    bases_e, up_e, cot_e, w_v, perm_v, permz_v, tab, xs, rin, hb, h5, hs, h_in, pre = take(14)
    gbuf, gpar, g5, g5p, bsum, dh_a, dh_b, gws, bias, gain = take(10)
    blocks, others, bias_blocks, bias_others = take(3), take(3), take(3), take(3)
    wres = next(names)
    local_sem, send_sem, recv_sem = take(3)

    pos, core, dp, seq = here()
    partner = place(pos, 1 - core)
    left, right = (dp, lax.rem(seq + 7, 8)), (dp, lax.rem(seq + 1, 8))
    inside = (seq > 0, seq < 7)

    def remote(n, src, dst, device):
        return pltpu.make_async_remote_copy(
            src_ref=src, dst_ref=dst, send_sem=send_sem.at[n], recv_sem=recv_sem.at[n],
            device_id=device, device_id_type=MESH,
        )

    def local(n, src, dst):
        return pltpu.make_async_copy(src, dst, local_sem.at[n])

    in_bases = local(0, bases, bases_e.at[:, pl.ds(128, ROWS)])
    in_up = local(1, up, up_e.at[pl.ds(HALO, ROWS)])
    in_row = [local(2, bias_in, bias.at[0]), local(3, gain_in, gain.at[0])]
    in_w = [local(6 + p, weight.at[:, pl.ds(p * WIDE, WIDE)], w_v.at[:, pl.ds(p * WIDE, WIDE)]) for p in range(GROUPS)]
    in_cot = local(9, cot, cot_e.at[pl.ds(HALO, ROWS)])
    for copy in (in_bases, in_up, *in_row, *in_w, in_cot):
        copy.start()

    barrier = pltpu.get_barrier_semaphore()
    partners = [partner, left, right]
    partners += [place(moved(pos, axis, delta), core) for axis in range(3) for delta in (1, 2, 3)]
    for device in partners:
        pl.semaphore_signal(barrier, inc=1, device_id=device, device_id_type=MESH)

    halos = [
        remote(0, bases.at[:, pl.ds(ROWS - 128, 128)], bases_e.at[:, pl.ds(0, 128)], right),
        remote(1, bases.at[:, pl.ds(0, 128)], bases_e.at[:, pl.ds(128 + ROWS, 128)], left),
    ]
    for n, (source, target) in enumerate(((up, up_e), (cot, cot_e))):
        halos += [
            remote(2 + 2 * n, source.at[pl.ds(ROWS - HALO, HALO)], target.at[pl.ds(0, HALO)], right),
            remote(3 + 2 * n, source.at[pl.ds(0, HALO)], target.at[pl.ds(HALO + ROWS, HALO)], left),
        ]
    h_copy = remote(6, hs.at[1], h_in, partner)

    def g_copy(p):
        return remote(7 + p, gbuf.at[p], gpar.at[p], partner)

    row = lax.broadcasted_iota(jnp.int32, (HALF, 128), 0)
    column = lax.broadcasted_iota(jnp.int32, (HALF, 128), 1)
    sixth = (row * 10923) >> 16
    last = row - 6 * sixth
    first, second, third = sixth >> 4, (sixth >> 2) & 3, sixth & 3
    channel = (first >> 1) * 384 + second * 96 + third * 12 + (first & 1) * 6 + last
    for n, c in enumerate((core, 1 - core)):
        for b in range(C // 128):
            hit = column + b * 128 == channel + c * 48
            perm_v[n * HALF : (n + 1) * HALF, b * 128 : (b + 1) * 128] = hit.astype(F32).astype(BF)
    kept = second * 96 + third * 24 + first * 6 + last
    for b in range(HALF // 128):
        permz_v[:, b * 128 : (b + 1) * 128] = (column + b * 128 == kept).astype(F32).astype(BF)

    tab[...] = jnp.zeros(tab.shape, F32)
    tab[0:4, :] = table[...].astype(F32)
    bsum[...] = jnp.zeros(bsum.shape, F32)
    code = lax.broadcasted_iota(jnp.int32, (8, 128), 0)

    def embedded(block):
        onehot = (code == bases_e[:, pl.ds(times(block, 128), 128)]).astype(F32)
        return lax.dot_general(onehot, tab[...], TN, preferred_element_type=F32)

    def normed_of(x):
        r = lax.rsqrt(jnp.mean(x * x, axis=-1, keepdims=True) + 1e-06)
        return r, (x * r * gain[...])

    def norm_block(b, carry):
        e = embedded(b + 1)
        for s in range(4):
            row = pl.multiple_of(b * 128 + s * 32, 32)
            x = up_e[pl.ds(row + HALO, 32), :].astype(F32) + e[s * 32 : s * 32 + 32]
            r, h = normed_of(x)
            xs[pl.ds(row, 32), :] = x
            rin[pl.ds(row, 32), :] = jnp.broadcast_to(r, (32, 128))
            hb[pl.ds(row + 2 * HALO, 32), :] = h.astype(BF)
        return carry

    def norm():
        for copy in (in_bases, in_up, *in_row):
            copy.wait()
        lax.fori_loop(0, ROWS // 128, norm_block, 0)
        pl.semaphore_wait(barrier, len(partners))
        for copy in halos:
            copy.start()

    def norm_ends():
        for copy in halos:
            copy.wait_recv()
        hb[0:HALO, :] = jnp.zeros((HALO, C), BF)
        hb[HALO + EXT : 2 * HALO + EXT, :] = jnp.zeros((HALO, C), BF)
        for side, (block, skip) in enumerate(((0, 128 - HALO), (1 + ROWS // 128, 0))):
            start = side * (HALO + ROWS)
            x = up_e[start : start + HALO, :].astype(F32) + embedded(block)[skip : skip + HALO]
            h = jnp.where(inside[side], normed_of(x)[1], 0.0)
            hb[start + HALO : start + 2 * HALO, :] = h.astype(BF)

    def turn():
        def one(n, carry):
            rows = perm_v[pl.ds(times(1 - n, HALF), HALF), :]
            h_own = hb[2 * HALO : 2 * HALO + ROWS, :]
            hs[1 - n] = lax.dot_general(rows, h_own, NT, preferred_element_type=F32).astype(BF)
            pl.when(n == 0)(h_copy.start)
            return carry

        lax.fori_loop(0, 2, one, 0)

    def shift_h():
        def tile(j, carry):
            row = times(j, 96)
            for p in range(GROUPS):
                v = hb[pl.ds(row, 128), p * WIDE : (p + 1) * WIDE].astype(F32)
                for k in range(TAPS):
                    h5[pl.ds(row, 96), k * C + p * WIDE : k * C + (p + 1) * WIDE] = v[8 + STEP * k : 104 + STEP * k].astype(BF)
            return carry

        lax.fori_loop(0, EXT // 96, tile, 0)

    c0 = np.float32(np.sqrt(2 / np.pi))

    def gelu_pair(z):
        square = z * z
        t = jnp.tanh(c0 * z * (1 + 0.044715 * square))
        cdf = 0.5 + 0.5 * t
        slope = cdf + (0.5 * c0) * z * (1 - t * t) * (1 + 0.134145 * square)
        return z * cdf, slope

    def forward(p):
        cols = pl.ds(times(p, WIDE), WIDE)
        for n in range(GROUPS):
            pl.when(p == n)(in_w[n].wait)
        pl.when(p == 0)(in_cot.wait)
        pre[...] = jnp.dot(h5[...], w_v[:, cols], preferred_element_type=F32)

        def tile(i, carry):
            row = times(i, 64)
            act, slope = gelu_pair(pre[pl.ds(row + HALO, 64), :] + bias[:, cols])
            ob[pl.ds(row, 64), cols] = (xs[pl.ds(row, 64), cols] + act).astype(BF)
            gbuf[p, pl.ds(row + HALO, 64), :] = (cot_e[pl.ds(row + HALO, 64), cols].astype(F32) * slope).astype(BF)
            return carry

        lax.fori_loop(0, ROWS // 64, tile, 0)
        for side in range(2):
            rows = slice(side * (HALO + ROWS), side * (HALO + ROWS) + HALO)
            _, slope = gelu_pair(pre[rows, :] + bias[:, cols])
            g = jnp.where(inside[side], cot_e[rows, cols].astype(F32) * slope, 0.0)
            gbuf[p, rows, :] = g.astype(BF)
        g_copy(p).start()

    def shift_g(source, p, target, column):
        def tile(j, total):
            row = times(j, 128)
            v = source[p, pl.ds(row, 160), :].astype(F32)
            for k in range(TAPS):
                target[pl.ds(row, 128), pl.ds(column(k), WIDE)] = v[24 - STEP * k : 152 - STEP * k].astype(BF)
            return total + jnp.sum(v[16:144].reshape(16, 8, WIDE), axis=0)

        bsum[:, pl.ds(times(p, WIDE), WIDE)] += lax.fori_loop(0, ROWS // 128, tile, jnp.zeros((8, WIDE), F32))

    def axis_of(kind, stage):
        return (kind, jnp.where(kind == 0, 1, 0), jnp.where(kind == 2, 1, 2))[stage]

    def along(axis):
        return jnp.where(axis == 0, pos[0], jnp.where(axis == 1, pos[1], pos[2]))

    def hops(first, axis, source, target):
        copies = []
        for delta in (1, 2, 3):
            other = [lax.rem(pos[a] + jnp.where(axis == a, delta, 0), 4) for a in range(3)]
            copies.append(remote(first + delta - 1, source(along(axis) + delta), target(delta - 1), place(other, core)))
        return copies

    def piece_hops(p, m, stage):
        slot, count = SLOTS[m]
        axis = axis_of(lax.rem(p + m, 3), stage)
        return hops(
            10 + ((p * 3 + m) * STAGES + stage) * 3,
            axis,
            lambda d: blocks[stage].at[p, lax.rem(d, 4), pl.ds(slot, count)],
            lambda d: others[stage].at[p, d, pl.ds(slot, count)],
        )

    def bias_hops(stage):
        return hops(
            10 + 27 * GROUPS + stage * 3,
            jnp.int32(stage),
            lambda d: bias_blocks[stage].at[lax.rem(d, 4)],
            lambda d: bias_others[stage].at[d],
        )

    def weights(p):
        shift_g(gbuf, p, g5, lambda k: pl.multiple_of(k * C + p * WIDE, WIDE))
        g_copy(p).wait_recv()
        shift_g(gpar, p, g5p, lambda k: TAP_OF.index(k) * WIDE)

        @pl.when(p == 0)
        def _():
            h_copy.wait_recv()

        def piece(m, first, count):
            own = [g5[:, pl.ds(pl.multiple_of(lax.rem(3 * (first + n), TAPS) * C + p * WIDE, WIDE), WIDE)] for n in range(count)]
            other = g5p[:, pl.ds(times(first, WIDE), count * WIDE)]
            rhs = jnp.concatenate([jnp.concatenate(own, axis=1) if count > 1 else own[0], other], axis=0)
            lhs = jnp.concatenate([hs[0], h_in[...]], axis=1)
            wres[:, 0 : count * WIDE] = jnp.dot(lhs, rhs, preferred_element_type=F32)
            kind = lax.rem(p + m, 3)
            for n in range(count):
                cols = slice(n * WIDE, (n + 1) * WIDE)

                def store(block):
                    for d in range(4):
                        blocks[0][p, d, first + n] = block(d).astype(BF)

                @pl.when(kind == 0)
                def _():
                    store(lambda d: wres[d * 96 : d * 96 + 96, cols])

                @pl.when(kind == 1)
                def _():
                    store(lambda d: jnp.concatenate([wres[e * 96 + d * 24 : e * 96 + d * 24 + 24, cols] for e in range(4)], axis=0))

                @pl.when(kind == 2)
                def _():
                    r = jnp.dot(permz_v[...], wres[:, cols].astype(BF), preferred_element_type=F32)
                    store(lambda d: r[d * 96 : d * 96 + 96])

        def pair(m, carry):
            piece(m, 2 * m, 2)
            for n in range(2):

                @pl.when(m == n)
                def _():
                    for copy in piece_hops(p, n, 0):
                        copy.start()

            return carry

        lax.fori_loop(0, 2, pair, 0)
        piece(2, 4, 1)
        for copy in piece_hops(p, 2, 0):
            copy.start()

        @pl.when(p == GROUPS - 1)
        def _():
            total = jnp.sum(bsum[...], axis=0, keepdims=True)
            total = jnp.broadcast_to(total, (128, C)).astype(BF)
            r = lax.dot_general(perm_v[0:HALF, :], total, NT, preferred_element_type=F32)
            for d in range(4):
                bias_blocks[0][d] = r[d * 96 : d * 96 + 96].astype(BF)
            for copy in bias_hops(0):
                copy.start()

    spread_row = lax.broadcasted_iota(jnp.int32, (64, 32), 0)
    spread_col = lax.broadcasted_iota(jnp.int32, (64, 32), 1)
    within = spread_row & 15
    spread = ((within < 6) & (spread_col == 6 * (spread_row >> 4) + within)).astype(F32).astype(BF)

    def handed_on(total, stage, store):
        if stage == 0:
            for d in range(4):
                block = jnp.concatenate([total[24 * d : 24 * d + 24], jnp.zeros((8, total.shape[1]), F32)], axis=0)
                store(d, block.astype(BF))
        else:
            r = jnp.dot(spread, total.astype(BF), preferred_element_type=F32).astype(BF)
            for d in range(4):
                store(d, r[16 * d : 16 * d + 16])

    def finish(p, stage):
        for m, (first, count) in enumerate(SLOTS):
            for copy in piece_hops(p, m, stage):
                copy.wait_recv()
            own = along(axis_of(lax.rem(p + m, 3), stage))
            for slot in range(first, first + count):
                total = blocks[stage][p, own, slot].astype(F32)
                for d in range(3):
                    total = total + others[stage][p, d, slot].astype(F32)
                if stage == 2:
                    gws[TAP_OF[slot], :, pl.ds(times(p, WIDE), WIDE)] = total[0:8]
                else:

                    def store(d, value):
                        blocks[stage + 1][p, d, slot] = value

                    handed_on(total, stage, store)
            if stage < 2:
                for copy in piece_hops(p, m, stage + 1):
                    copy.start()

    def finish_bias(stage):
        for copy in bias_hops(stage):
            copy.wait_recv()
        total = bias_blocks[stage][pos[stage]].astype(F32)
        for d in range(3):
            total = total + bias_others[stage][d].astype(F32)
        if stage == 2:
            gws[TAPS, :, 0:128] = total[0:8]
        else:

            def store(d, value):
                bias_blocks[stage + 1][d] = value

            handed_on(total, stage, store)
            for copy in bias_hops(stage + 1):
                copy.start()

    def hidden(t):
        rows = pl.ds(times(t, TILE), TILE)
        return sum(
            lax.dot_general(g5[rows, k * C : (k + 1) * C], w_v[k * C : (k + 1) * C, :], NT, preferred_element_type=F32)
            for k in range(TAPS)
        )

    def input_gradient(t, dh):
        for i in range(TILE // 32):
            row = pl.multiple_of(t * TILE + i * 32, 32)
            r = jnp.concatenate([rin[pl.ds(row, 32), :]] * (C // 128), axis=1)
            normed = xs[pl.ds(row, 32), :] * r
            dn = dh[i * 32 : i * 32 + 32, :] * gain[...]
            mean = jnp.mean(dn * normed, axis=-1, keepdims=True)
            g = cot_e[pl.ds(row + HALO, 32), :].astype(F32) + (dn - normed * mean) * r
            gi[pl.ds(row, 32), :] = g.astype(BF)

    def backward(u):
        dh_a[...] = hidden(2 * u)
        input_gradient(jnp.maximum(2 * u - 1, 0), dh_b)
        dh_b[...] = hidden(2 * u + 1)
        input_gradient(2 * u, dh_a)

    def during(s, start, stop, step):
        if stop > start:
            pl.when((s >= start) & (s < stop))(step)

    def turn_of(s, carry):
        during(s, 0, 3, lambda: forward(s))
        during(s, 1, 4, lambda: weights(s - 1))
        during(s, 4, 6, lambda: backward(s - 4))
        for stage in range(STAGES):
            during(s, 2 + stage, 5 + stage, lambda: finish(s - 2 - stage, stage))
            during(s, 4 + stage, 5 + stage, lambda: finish_bias(stage))
        return carry

    norm()
    turn()
    norm_ends()
    shift_h()
    dh_b[...] = jnp.zeros(dh_b.shape, F32)
    lax.fori_loop(0, 6, turn_of, 0)
    input_gradient(ROWS // TILE - 1, dh_b)
    finish(2, 2)
    finish_bias(2)

    gw[...] = gws[0:TAPS, 0:6, :]
    mine = (dp * 8 + seq) * 6
    base = jnp.minimum(lax.div(mine, 16) * 16, C - 32)
    pick_row = lax.broadcasted_iota(jnp.int32, (8, 32), 0)
    pick_col = lax.broadcasted_iota(jnp.int32, (8, 32), 1)
    pick = (pick_col == pick_row + (mine - base)).astype(F32).astype(BF)
    total = jnp.zeros((8, C), F32)
    for k in range(TAPS):
        rows = w_v[pl.ds(pl.multiple_of(k * C + base, 16), 32), :]
        total = total + jnp.dot(pick, rows, preferred_element_type=F32) * gws[k]
    lane = lax.broadcasted_iota(jnp.int32, (8, C), 1)
    row = lax.broadcasted_iota(jnp.int32, (8, C), 0)
    own_gain = jnp.sum(jnp.where(lane == row + mine, gain[...], 0.0), axis=-1, keepdims=True)
    column = jnp.sum(total, axis=-1, keepdims=True) / own_gain
    diagonal = (lane == row)[:, 0:128] & (row < 6)[:, 0:128]
    small[0:1, :] = jnp.sum(jnp.where(diagonal, gws[TAPS, :, 0:128], 0.0), axis=0, keepdims=True)
    small[1:2, :] = jnp.sum(jnp.where(diagonal, column, 0.0), axis=0, keepdims=True)

    for copy in (*halos, h_copy):
        copy.wait_send()
    for stage in range(STAGES):
        for copy in bias_hops(stage):
            copy.wait_send()

    def sent(p, carry):
        g_copy(p).wait_send()
        for m in range(3):
            for stage in range(STAGES):
                for copy in piece_hops(p, m, stage):
                    copy.wait_send()
        return carry

    lax.fori_loop(0, GROUPS, sent, 0)


MESH = pl.DeviceIdType.MESH


def body(bases, upsampled, base_table, filter_weight, filter_bias, norm_gain, cotangent):
    vmem, hbm = pl.BlockSpec(memory_space=pltpu.VMEM), pl.BlockSpec(memory_space=pl.ANY)
    scratch = [
        pltpu.VMEM((1, ROWS + 256), jnp.int32),
        pltpu.VMEM((EXT, C), BF),
        pltpu.VMEM((EXT, C), BF),
        pltpu.VMEM((TAPS * C, C), BF),
        pltpu.VMEM((C, C), BF),
        pltpu.VMEM((HALF, HALF), BF),
        pltpu.VMEM((8, C), F32),
        pltpu.VMEM((ROWS, C), F32),
        pltpu.VMEM((ROWS, 128), F32),
        pltpu.VMEM((EXT + 2 * HALO, C), BF),
        pltpu.VMEM((EXT, TAPS * C), BF),
        pltpu.VMEM((2, HALF, ROWS), BF),
        pltpu.VMEM((HALF, ROWS), BF),
        pltpu.VMEM((EXT, WIDE), F32),
        pltpu.VMEM((GROUPS, EXT, WIDE), BF),
        pltpu.VMEM((GROUPS, EXT, WIDE), BF),
        pltpu.VMEM((ROWS, TAPS * C), BF),
        pltpu.VMEM((ROWS, TAPS * WIDE), BF),
        pltpu.VMEM((8, C), F32),
        pltpu.VMEM((TILE, C), F32),
        pltpu.VMEM((TILE, C), F32),
        pltpu.VMEM((TAPS + 1, 8, C), F32),
        pltpu.VMEM((1, C), F32),
        pltpu.VMEM((1, C), F32),
    ]
    scratch += [pltpu.VMEM((GROUPS, 4, TAPS, rows, WIDE), BF) for rows in BLOCK_ROWS]
    scratch += [pltpu.VMEM((GROUPS, 3, TAPS, rows, WIDE), BF) for rows in BLOCK_ROWS]
    scratch += [pltpu.VMEM((4, rows, 128), BF) for rows in BLOCK_ROWS]
    scratch += [pltpu.VMEM((3, rows, 128), BF) for rows in BLOCK_ROWS]
    scratch += [pltpu.VMEM((HALF, 2 * WIDE), F32)]
    remotes = 10 + 27 * GROUPS + 9
    scratch += [
        pltpu.SemaphoreType.DMA((16,)),
        pltpu.SemaphoreType.DMA((remotes,)),
        pltpu.SemaphoreType.DMA((remotes,)),
    ]
    out, gin, gw, small = pl.pallas_call(
        kernel,
        out_shape=[
            pltpu.VMEM((ROWS, C), BF),
            pltpu.VMEM((ROWS, C), BF),
            pltpu.VMEM((TAPS, 6, C), F32),
            pltpu.VMEM((8, 128), F32),
        ],
        in_specs=[hbm, hbm, vmem, hbm, hbm, hbm, hbm],
        out_specs=[vmem, vmem, vmem, vmem],
        scratch_shapes=scratch,
        compiler_params=pltpu.CompilerParams(collective_id=0, has_side_effects=True, vmem_limit_bytes=58 * 2**20),
        name="block",
    )(
        bases,
        upsampled[0],
        base_table,
        filter_weight.reshape(TAPS * C, C),
        filter_bias,
        norm_gain,
        cotangent[0],
    )
    return out[None], gin[None], gw, small[0, 0:6], small[1, 0:6]


def solution(mesh):
    placed = (P("dp", "seq"), P("dp", "seq", None), P(), P(), P(), P(), P("dp", "seq", None))
    return jax.shard_map(
        body,
        mesh=mesh,
        in_specs=placed,
        out_specs=(
            P("dp", "seq", None),
            P("dp", "seq", None),
            P(None, ("dp", "seq"), None),
            P(("dp", "seq")),
            P(("dp", "seq")),
        ),
        check_vma=False,
    )
```

```python
import jax
import jax.numpy as jnp
import numpy as np
from jax import lax
from jax.experimental import pallas as pl
from jax.experimental.pallas import tpu as pltpu
from jax.sharding import PartitionSpec as P

BF, F32 = jnp.bfloat16, jnp.float32
C, TAPS, STEP = 768, 5, 4
ROWS, HALO = 1024, 16
EXT = ROWS + 2 * HALO
WIDE = 256
GROUPS = C // WIDE
HALF = C // 2
NT = (((1,), (1,)), ((), ()))
TN = (((0,), (0,)), ((), ()))

TAP_OF = [3 * slot % TAPS for slot in range(TAPS)]
SLOTS = ((0, 2), (2, 2), (4, 1))
STAGES = 3
KEPT = ((0, 2, 3, 1), (0, 1, 2, 3))
TILE = 256
BLOCK_ROWS = (96, 32, 16)


def here():
    dp, seq = lax.axis_index("dp"), lax.axis_index("seq")
    x = 2 * lax.div(dp, 8) + lax.rem(seq, 2)
    return [x, lax.rem(lax.div(dp, 2), 4), lax.div(seq, 2)], lax.rem(dp, 2), dp, seq


def place(pos, core):
    x, y, z = pos
    return (lax.div(x, 2) * 8 + y * 2 + core, z * 2 + lax.rem(x, 2))


def moved(pos, axis, delta):
    other = list(pos)
    other[axis] = lax.rem(pos[axis] + delta, 4)
    return other


def times(value, step):
    return pl.multiple_of(value * step, step)


def kernel(*refs):
    names = iter(refs)

    def take(n):
        return [next(names) for _ in range(n)]

    bases, up, table, weight, bias_in, gain_in, cot = take(7)
    ob, gi, gw, small = take(4)
    bases_e, up_e, cot_e, w_v, perm_v, permz_v, tab, xs, rin, hb, h5, hs, h_in, pre = take(14)
    gbuf, gpar, g5, g5p, bsum, dh, gws, bias, gain = take(9)
    first_own, first_in, second_own, second_in = take(4)
    blocks, others, bias_blocks, bias_others = [None, *take(2)], [None, *take(2)], take(3), take(3)
    wres = next(names)
    local_sem, send_sem, recv_sem = take(3)

    pos, core, dp, seq = here()
    partner = place(pos, 1 - core)
    left, right = (dp, lax.rem(seq + 7, 8)), (dp, lax.rem(seq + 1, 8))
    inside = (seq > 0, seq < 7)

    def remote(n, src, dst, device):
        return pltpu.make_async_remote_copy(
            src_ref=src, dst_ref=dst, send_sem=send_sem.at[n], recv_sem=recv_sem.at[n],
            device_id=device, device_id_type=MESH,
        )

    def local(n, src, dst):
        return pltpu.make_async_copy(src, dst, local_sem.at[n])

    in_bases = local(0, bases, bases_e.at[:, pl.ds(128, ROWS)])
    in_up = local(1, up, up_e.at[pl.ds(HALO, ROWS)])
    in_row = [local(2, bias_in, bias.at[0]), local(3, gain_in, gain.at[0])]
    in_w = [local(6 + p, weight.at[:, pl.ds(p * WIDE, WIDE)], w_v.at[:, pl.ds(p * WIDE, WIDE)]) for p in range(GROUPS)]
    in_cot = local(9, cot, cot_e.at[pl.ds(HALO, ROWS)])
    for copy in (in_bases, in_up, *in_row, *in_w, in_cot):
        copy.start()

    barrier = pltpu.get_barrier_semaphore()
    partners = [partner, left, right]
    partners += [place(moved(pos, axis, delta), core) for axis in range(3) for delta in (1, 2, 3)]
    for device in partners:
        pl.semaphore_signal(barrier, inc=1, device_id=device, device_id_type=MESH)

    halos = [
        remote(0, bases.at[:, pl.ds(ROWS - 128, 128)], bases_e.at[:, pl.ds(0, 128)], right),
        remote(1, bases.at[:, pl.ds(0, 128)], bases_e.at[:, pl.ds(128 + ROWS, 128)], left),
    ]
    for n, (source, target) in enumerate(((up, up_e), (cot, cot_e))):
        halos += [
            remote(2 + 2 * n, source.at[pl.ds(ROWS - HALO, HALO)], target.at[pl.ds(0, HALO)], right),
            remote(3 + 2 * n, source.at[pl.ds(0, HALO)], target.at[pl.ds(HALO + ROWS, HALO)], left),
        ]
    h_copy = remote(6, hs.at[1], h_in, partner)

    def g_copy(p):
        return remote(7 + p, gbuf.at[p], gpar.at[p], partner)

    row = lax.broadcasted_iota(jnp.int32, (HALF, 128), 0)
    column = lax.broadcasted_iota(jnp.int32, (HALF, 128), 1)
    sixth = (row * 10923) >> 16
    last = row - 6 * sixth
    first, second, third = sixth >> 4, (sixth >> 2) & 3, sixth & 3
    channel = (first >> 1) * 384 + second * 96 + third * 12 + (first & 1) * 6 + last
    for n, c in enumerate((core, 1 - core)):
        for b in range(C // 128):
            hit = column + b * 128 == channel + c * 48
            perm_v[n * HALF : (n + 1) * HALF, b * 128 : (b + 1) * 128] = hit.astype(F32).astype(BF)
    turned = second * 96 + third * 24 + first * 6 + last
    for b in range(HALF // 128):
        permz_v[:, b * 128 : (b + 1) * 128] = (column + b * 128 == turned).astype(F32).astype(BF)

    tab[...] = jnp.zeros(tab.shape, F32)
    tab[0:4, :] = table[...].astype(F32)
    bsum[...] = jnp.zeros(bsum.shape, F32)
    code = lax.broadcasted_iota(jnp.int32, (8, 128), 0)

    def embedded(block):
        onehot = (code == bases_e[:, pl.ds(times(block, 128), 128)]).astype(F32)
        return lax.dot_general(onehot, tab[...], TN, preferred_element_type=F32)

    def normed_of(x):
        r = lax.rsqrt(jnp.mean(x * x, axis=-1, keepdims=True) + 1e-06)
        return r, (x * r * gain[...])

    def norm_block(pair, carry):
        both = [embedded(2 * pair + 1), embedded(2 * pair + 2)]
        for s in range(8):
            row = pl.multiple_of(pair * 256 + s * 32, 32)
            x = up_e[pl.ds(row + HALO, 32), :].astype(F32) + both[s // 4][s % 4 * 32 : s % 4 * 32 + 32]
            r, h = normed_of(x)
            xs[pl.ds(row, 32), :] = x
            rin[pl.ds(row, 32), :] = jnp.broadcast_to(r, (32, 128))
            hb[pl.ds(row + 2 * HALO, 32), :] = h.astype(BF)
        return carry

    def norm():
        for copy in (in_bases, in_up, *in_row):
            copy.wait()
        lax.fori_loop(0, ROWS // 256, norm_block, 0)
        pl.semaphore_wait(barrier, len(partners))
        for copy in halos:
            copy.start()

    def norm_ends():
        for copy in halos:
            copy.wait_recv()
        hb[0:HALO, :] = jnp.zeros((HALO, C), BF)
        hb[HALO + EXT : 2 * HALO + EXT, :] = jnp.zeros((HALO, C), BF)
        for side, (block, skip) in enumerate(((0, 128 - HALO), (1 + ROWS // 128, 0))):
            start = side * (HALO + ROWS)
            x = up_e[start : start + HALO, :].astype(F32) + embedded(block)[skip : skip + HALO]
            h = jnp.where(inside[side], normed_of(x)[1], 0.0)
            hb[start + HALO : start + 2 * HALO, :] = h.astype(BF)

    def turn():
        def one(n, carry):
            rows = perm_v[pl.ds(times(1 - n, HALF), HALF), :]
            h_own = hb[2 * HALO : 2 * HALO + ROWS, :]
            hs[1 - n] = lax.dot_general(rows, h_own, NT, preferred_element_type=F32).astype(BF)
            pl.when(n == 0)(h_copy.start)
            return carry

        lax.fori_loop(0, 2, one, 0)

    def shift_h():
        def tile(j, carry):
            row = times(j, 96)
            for p in range(GROUPS):
                v = hb[pl.ds(row, 128), p * WIDE : (p + 1) * WIDE].astype(F32)
                for k in range(TAPS):
                    h5[pl.ds(row, 96), k * C + p * WIDE : k * C + (p + 1) * WIDE] = v[8 + STEP * k : 104 + STEP * k].astype(BF)
            return carry

        lax.fori_loop(0, EXT // 96, tile, 0)

    c0 = np.float32(np.sqrt(2 / np.pi))

    def gelu_pair(z):
        square = z * z
        t = jnp.tanh(c0 * z * (1 + 0.044715 * square))
        cdf = 0.5 + 0.5 * t
        slope = cdf + (0.5 * c0) * z * (1 - t * t) * (1 + 0.134145 * square)
        return z * cdf, slope

    def forward(p):
        cols = pl.ds(times(p, WIDE), WIDE)
        for n in range(GROUPS):
            pl.when(p == n)(in_w[n].wait)
        pl.when(p == 0)(in_cot.wait)
        half = EXT // 2

        def tile(row, n):
            act, slope = gelu_pair(pre[row + HALO : row + HALO + n, :] + bias[:, cols])
            ob[row : row + n, cols] = (xs[row : row + n, cols] + act).astype(BF)
            gbuf[p, row + HALO : row + HALO + n, :] = (cot_e[row + HALO : row + HALO + n, cols].astype(F32) * slope).astype(BF)

        pre[0:half, :] = jnp.dot(h5[0:half, :], w_v[:, cols], preferred_element_type=F32)
        for row in range(0, half - HALO, 64):
            tile(row, 64)
        pre[half:, :] = jnp.dot(h5[half:, :], w_v[:, cols], preferred_element_type=F32)
        for row in range(half - HALO, ROWS, 64):
            tile(row, 64)
        for side in range(2):
            rows = slice(side * (HALO + ROWS), side * (HALO + ROWS) + HALO)
            _, slope = gelu_pair(pre[rows, :] + bias[:, cols])
            g = jnp.where(inside[side], cot_e[rows, cols].astype(F32) * slope, 0.0)
            gbuf[p, rows, :] = g.astype(BF)
        g_copy(p).start()

    def shift_g(source, p, target, column):
        def tile(j, total):
            row = times(j, 128)
            v = source[p, pl.ds(row, 160), :].astype(F32)
            for k in range(TAPS):
                target[pl.ds(row, 128), pl.ds(column(k), WIDE)] = v[24 - STEP * k : 152 - STEP * k].astype(BF)
            return total + jnp.sum(v[16:144].reshape(16, 8, WIDE), axis=0)

        bsum[:, pl.ds(times(p, WIDE), WIDE)] += lax.fori_loop(0, ROWS // 128, tile, jnp.zeros((8, WIDE), F32))

    def axis_of(kind, stage):
        return (kind, jnp.where(kind == 0, 1, 0), jnp.where(kind == 2, 1, 2))[stage]

    def along(axis):
        return jnp.where(axis == 0, pos[0], jnp.where(axis == 1, pos[1], pos[2]))

    def hops(first, axis, source, target):
        copies = []
        for delta in (1, 2, 3):
            other = [lax.rem(pos[a] + jnp.where(axis == a, delta, 0), 4) for a in range(3)]
            copies.append(remote(first + delta - 1, source(along(axis) + delta), target(delta - 1), place(other, core)))
        return copies

    def kept_set(c, odd):
        return c >> 1 if odd else ((c + 1) >> 1) & 1

    def mine_of(c, odd):
        return c & 1 if odd else c >> 1

    def pair_copy(p, slot, odd, step):
        kind = lax.rem(p + lax.div(slot, 2), 3)
        c = along(kind)
        to = c ^ 1 if (step == 1) == odd else 3 - c
        other = [jnp.where(kind == a, to, pos[a]) for a in range(3)]
        n = 10 + (p * TAPS + slot) * 2 + step
        if step == 0:
            source = first_own.at[p, slot, pl.ds(2 * kept_set(to, odd), 2)]
            return remote(n, source, first_in.at[p, slot], place(other, core))
        return remote(n, second_own.at[p, slot], second_in.at[p, slot], place(other, core))

    def piece_hops(p, m, stage):
        slot, count = SLOTS[m]
        axis = axis_of(lax.rem(p + m, 3), stage)
        return hops(
            40 + ((p * 3 + m) * 2 + stage - 1) * 3,
            axis,
            lambda d: blocks[stage].at[p, lax.rem(d, 4), pl.ds(slot, count)],
            lambda d: others[stage].at[p, d, pl.ds(slot, count)],
        )

    def bias_hops(stage):
        return hops(
            10 + 28 * GROUPS + stage * 3,
            jnp.int32(stage),
            lambda d: bias_blocks[stage].at[lax.rem(d, 4)],
            lambda d: bias_others[stage].at[d],
        )

    def weights(p):
        shift_g(gbuf, p, g5, lambda k: pl.multiple_of(k * C + p * WIDE, WIDE))
        g_copy(p).wait_recv()
        shift_g(gpar, p, g5p, lambda k: TAP_OF.index(k) * WIDE)

        @pl.when(p == 0)
        def _():
            h_copy.wait_recv()

        def piece(m, first, count):
            own = [g5[:, pl.ds(pl.multiple_of(lax.rem(3 * (first + n), TAPS) * C + p * WIDE, WIDE), WIDE)] for n in range(count)]
            other = g5p[:, pl.ds(times(first, WIDE), count * WIDE)]
            rhs = jnp.concatenate([jnp.concatenate(own, axis=1) if count > 1 else own[0], other], axis=0)
            lhs = jnp.concatenate([hs[0], h_in[...]], axis=1)
            wres[:, 0 : count * WIDE] = jnp.dot(lhs, rhs, preferred_element_type=F32)
            kind = lax.rem(p + m, 3)
            wide = count * WIDE

            def store(block):
                for d in range(4):
                    rows = block(d).astype(BF)
                    for n in range(count):
                        first_own[p, first + n, KEPT[n][d]] = rows[:, n * WIDE : (n + 1) * WIDE]

            @pl.when(kind == 0)
            def _():
                store(lambda d: wres[d * 96 : d * 96 + 96, 0:wide])

            @pl.when(kind == 1)
            def _():
                store(lambda d: jnp.concatenate([wres[e * 96 + d * 24 : e * 96 + d * 24 + 24, 0:wide] for e in range(4)], axis=0))

            @pl.when(kind == 2)
            def _():
                r = jnp.dot(permz_v[...], wres[:, 0:wide].astype(BF), preferred_element_type=F32)
                store(lambda d: r[d * 96 : d * 96 + 96])

            for n in range(count):
                pair_copy(p, first + n, n, 0).start()

        def pair(m, carry):
            piece(m, 2 * m, 2)
            return carry

        lax.fori_loop(0, 2, pair, 0)
        piece(2, 4, 1)

        @pl.when(p == GROUPS - 1)
        def _():
            total = jnp.sum(bsum[...], axis=0, keepdims=True)
            total = jnp.broadcast_to(total, (128, C)).astype(BF)
            r = lax.dot_general(perm_v[0:HALF, :], total, NT, preferred_element_type=F32)
            for d in range(4):
                bias_blocks[0][d] = r[d * 96 : d * 96 + 96].astype(BF)
            for copy in bias_hops(0):
                copy.start()

    def spread_of(shape, sixteenth):
        r, c = lax.broadcasted_iota(jnp.int32, shape, 0), lax.broadcasted_iota(jnp.int32, shape, 1)
        return sixteenth(c, 6 * (r >> 4), r & 15).astype(F32).astype(BF)

    spread = spread_of((64, 32), lambda c, base, w: (w < 6) & (c == base + w))
    spread_two = spread_of((64, 48), lambda c, base, w: ((w & 7) < 6) & (c == base + (w & 7) + 24 * (w >> 3)))

    def handed_on(total, stage, store):
        if stage == 0:
            for d in range(4):
                block = jnp.concatenate([total[24 * d : 24 * d + 24], jnp.zeros((8, total.shape[1]), F32)], axis=0)
                store(d, block.astype(BF))
        else:
            r = jnp.dot(spread, total.astype(BF), preferred_element_type=F32).astype(BF)
            for d in range(4):
                store(d, r[16 * d : 16 * d + 16])

    def finish_first(p, step):
        for m, (first, count) in enumerate(SLOTS):
            c = along(lax.rem(p + m, 3))
            for slot in range(first, first + count):
                odd = slot % 2
                pair_copy(p, slot, odd, step).wait_recv()
                mine = mine_of(c, odd)
                if step == 0:
                    mine = 1 - mine
                total = first_own[p, slot, 2 * kept_set(c, odd) + mine].astype(F32) + first_in[p, slot, mine].astype(F32)
                if step == 0:
                    second_own[p, slot, 0] = total.astype(BF)
                    pair_copy(p, slot, odd, 1).start()
                else:
                    total = total + second_in[p, slot, 0].astype(F32)
                    for d in range(4):
                        rows = total[24 * d : 24 * d + 24]
                        block = jnp.concatenate([rows[:, 0:128], rows[:, 128:]], axis=0)
                        blocks[1][p, d, slot] = block.astype(BF)
            if step == 1:
                for copy in piece_hops(p, m, 1):
                    copy.start()

    def finish_next(p, stage):
        for m, (first, count) in enumerate(SLOTS):
            for copy in piece_hops(p, m, stage):
                copy.wait_recv()
            own = along(axis_of(lax.rem(p + m, 3), stage))
            for slot in range(first, first + count):
                total = blocks[stage][p, own, slot].astype(F32)
                for d in range(3):
                    total = total + others[stage][p, d, slot].astype(F32)
                if stage == 1:
                    r = jnp.dot(spread_two, total.astype(BF), preferred_element_type=F32).astype(BF)
                    for d in range(4):
                        blocks[2][p, d, slot] = r[16 * d : 16 * d + 16]
                else:
                    for half in range(2):
                        gws[TAP_OF[slot], :, pl.ds(times(2 * p + half, 128), 128)] = total[8 * half : 8 * half + 8]
            if stage == 1:
                for copy in piece_hops(p, m, 2):
                    copy.start()

    def finish(p, step):
        if step < 2:
            finish_first(p, step)
        else:
            finish_next(p, step - 1)

    def finish_bias(stage):
        for copy in bias_hops(stage):
            copy.wait_recv()
        total = bias_blocks[stage][pos[stage]].astype(F32)
        for d in range(3):
            total = total + bias_others[stage][d].astype(F32)
        if stage == 2:
            gws[TAPS, :, 0:128] = total[0:8]
        else:

            def store(d, value):
                bias_blocks[stage + 1][d] = value

            handed_on(total, stage, store)
            for copy in bias_hops(stage + 1):
                copy.start()

    def hidden(t):
        rows = pl.ds(times(t, TILE), TILE)
        return sum(
            lax.dot_general(g5[rows, k * C : (k + 1) * C], w_v[k * C : (k + 1) * C, :], NT, preferred_element_type=F32)
            for k in range(TAPS)
        )

    def input_gradient(t):
        for i in range(TILE // 32):
            row = pl.multiple_of(t * TILE + i * 32, 32)
            r = jnp.concatenate([rin[pl.ds(row, 32), :]] * (C // 128), axis=1)
            normed = xs[pl.ds(row, 32), :] * r
            dn = dh[i * 32 : i * 32 + 32, :] * gain[...]
            mean = jnp.mean(dn * normed, axis=-1, keepdims=True)
            g = cot_e[pl.ds(row + HALO, 32), :].astype(F32) + (dn - normed * mean) * r
            gi[pl.ds(row, 32), :] = g.astype(BF)

    def backward(t):
        input_gradient(jnp.maximum(t - 1, 0))
        dh[...] = hidden(t)

    def during(s, start, stop, step):
        if stop > start:
            pl.when((s >= start) & (s < stop))(step)

    def turn_of(s, carry):
        during(s, 0, 3, lambda: forward(s))
        during(s, 1, 4, lambda: weights(s - 1))
        during(s, 4, 8, lambda: backward(s - 4))
        for step in range(4):
            during(s, 2 + step, 5 + step, lambda: finish(s - 2 - step, step))
            if step < 3:
                during(s, 5 + step, 6 + step, lambda: finish_bias(step))
        return carry

    norm()
    turn()
    norm_ends()
    shift_h()
    dh[...] = jnp.zeros(dh.shape, F32)
    lax.fori_loop(0, 8, turn_of, 0)
    input_gradient(ROWS // TILE - 1)

    gw[...] = gws[0:TAPS, 0:6, :]
    mine = (dp * 8 + seq) * 6
    base = jnp.minimum(lax.div(mine, 16) * 16, C - 32)
    pick_row = lax.broadcasted_iota(jnp.int32, (8, 32), 0)
    pick_col = lax.broadcasted_iota(jnp.int32, (8, 32), 1)
    pick = (pick_col == pick_row + (mine - base)).astype(F32).astype(BF)
    total = jnp.zeros((8, C), F32)
    for k in range(TAPS):
        rows = w_v[pl.ds(pl.multiple_of(k * C + base, 16), 32), :]
        total = total + jnp.dot(pick, rows, preferred_element_type=F32) * gws[k]
    lane = lax.broadcasted_iota(jnp.int32, (8, C), 1)
    row = lax.broadcasted_iota(jnp.int32, (8, C), 0)
    own_gain = jnp.sum(jnp.where(lane == row + mine, gain[...], 0.0), axis=-1, keepdims=True)
    column = jnp.sum(total, axis=-1, keepdims=True) / own_gain
    diagonal = (lane == row)[:, 0:128] & (row < 6)[:, 0:128]
    small[0:1, :] = jnp.sum(jnp.where(diagonal, gws[TAPS, :, 0:128], 0.0), axis=0, keepdims=True)
    small[1:2, :] = jnp.sum(jnp.where(diagonal, column, 0.0), axis=0, keepdims=True)

    for copy in (*halos, h_copy):
        copy.wait_send()
    for stage in range(STAGES):
        for copy in bias_hops(stage):
            copy.wait_send()

    def sent(p, carry):
        g_copy(p).wait_send()
        for slot in range(TAPS):
            for step in range(2):
                pair_copy(p, slot, slot % 2, step).wait_send()
        for m in range(3):
            for stage in (1, 2):
                for copy in piece_hops(p, m, stage):
                    copy.wait_send()
        return carry

    lax.fori_loop(0, GROUPS, sent, 0)


MESH = pl.DeviceIdType.MESH


def body(bases, upsampled, base_table, filter_weight, filter_bias, norm_gain, cotangent):
    vmem, hbm = pl.BlockSpec(memory_space=pltpu.VMEM), pl.BlockSpec(memory_space=pl.ANY)
    scratch = [
        pltpu.VMEM((1, ROWS + 256), jnp.int32),
        pltpu.VMEM((EXT, C), BF),
        pltpu.VMEM((EXT, C), BF),
        pltpu.VMEM((TAPS * C, C), BF),
        pltpu.VMEM((C, C), BF),
        pltpu.VMEM((HALF, HALF), BF),
        pltpu.VMEM((8, C), F32),
        pltpu.VMEM((ROWS, C), F32),
        pltpu.VMEM((ROWS, 128), F32),
        pltpu.VMEM((EXT + 2 * HALO, C), BF),
        pltpu.VMEM((EXT, TAPS * C), BF),
        pltpu.VMEM((2, HALF, ROWS), BF),
        pltpu.VMEM((HALF, ROWS), BF),
        pltpu.VMEM((EXT, WIDE), F32),
        pltpu.VMEM((GROUPS, EXT, WIDE), BF),
        pltpu.VMEM((GROUPS, EXT, WIDE), BF),
        pltpu.VMEM((ROWS, TAPS * C), BF),
        pltpu.VMEM((ROWS, TAPS * WIDE), BF),
        pltpu.VMEM((8, C), F32),
        pltpu.VMEM((TILE, C), F32),
        pltpu.VMEM((TAPS + 1, 8, C), F32),
        pltpu.VMEM((1, C), F32),
        pltpu.VMEM((1, C), F32),
    ]
    scratch += [pltpu.VMEM((GROUPS, TAPS, n, 96, WIDE), BF) for n in (4, 2, 1, 1)]
    scratch += [pltpu.VMEM((GROUPS, 4, TAPS, rows, 128), BF) for rows in (48, 16)]
    scratch += [pltpu.VMEM((GROUPS, 3, TAPS, rows, 128), BF) for rows in (48, 16)]
    scratch += [pltpu.VMEM((4, rows, 128), BF) for rows in BLOCK_ROWS]
    scratch += [pltpu.VMEM((3, rows, 128), BF) for rows in BLOCK_ROWS]
    scratch += [pltpu.VMEM((HALF, 2 * WIDE), F32)]
    remotes = 10 + 28 * GROUPS + 9
    scratch += [
        pltpu.SemaphoreType.DMA((16,)),
        pltpu.SemaphoreType.DMA((remotes,)),
        pltpu.SemaphoreType.DMA((remotes,)),
    ]
    out, gin, gw, small = pl.pallas_call(
        kernel,
        out_shape=[
            pltpu.VMEM((ROWS, C), BF),
            pltpu.VMEM((ROWS, C), BF),
            pltpu.VMEM((TAPS, 6, C), F32),
            pltpu.VMEM((8, 128), F32),
        ],
        in_specs=[hbm, hbm, vmem, hbm, hbm, hbm, hbm],
        out_specs=[vmem, vmem, vmem, vmem],
        scratch_shapes=scratch,
        compiler_params=pltpu.CompilerParams(collective_id=0, has_side_effects=True, vmem_limit_bytes=58 * 2**20),
        name="block",
    )(
        bases,
        upsampled[0],
        base_table,
        filter_weight.reshape(TAPS * C, C),
        filter_bias,
        norm_gain,
        cotangent[0],
    )
    return out[None], gin[None], gw, small[0, 0:6], small[1, 0:6]


def solution(mesh):
    placed = (P("dp", "seq"), P("dp", "seq", None), P(), P(), P(), P(), P("dp", "seq", None))
    return jax.shard_map(
        body,
        mesh=mesh,
        in_specs=placed,
        out_specs=(
            P("dp", "seq", None),
            P("dp", "seq", None),
            P(None, ("dp", "seq"), None),
            P(("dp", "seq")),
            P(("dp", "seq")),
        ),
        check_vma=False,
    )
```

```python
import jax
import jax.numpy as jnp
import numpy as np
from jax import lax
from jax.experimental import pallas as pl
from jax.experimental.pallas import tpu as pltpu
from jax.sharding import PartitionSpec as P

BF, F32 = jnp.bfloat16, jnp.float32
C, TAPS, STEP = 768, 5, 4
ROWS, HALO = 1024, 16
EXT = ROWS + 2 * HALO
WIDE = 256
GROUPS = C // WIDE
HALF = C // 2
NT = (((1,), (1,)), ((), ()))
TN = (((0,), (0,)), ((), ()))

TAP_OF = [3 * slot % TAPS for slot in range(TAPS)]
SLOTS = ((0, 2), (2, 2), (4, 1))
STAGES = 3
KEPT = ((0, 2, 3, 1), (0, 1, 2, 3))
TILE = 256
BLOCK_ROWS = (96, 32, 16)


def here():
    dp, seq = lax.axis_index("dp"), lax.axis_index("seq")
    return [2 * (dp >> 3) + (seq & 1), (dp >> 1) & 3, seq >> 1], dp & 1, dp, seq


def place(pos, core):
    x, y, z = pos
    return ((x >> 1) * 8 + y * 2 + core, z * 2 + (x & 1))


def moved(pos, axis, to):
    other = list(pos)
    other[axis] = to
    return other


def times(value, step):
    return pl.multiple_of(value * step, step)


def kernel(*refs):
    names = iter(refs)

    def take(n):
        return [next(names) for _ in range(n)]

    bases, up, table, weight, bias_in, gain_in, cot = take(7)
    ob, gi, gw, small = take(4)
    bases_e, up_e, cot_e, w_v, perm_v, permz_v, tab, xs, rin, hb, h5, hs, h_in, pre = take(14)
    gbuf, gpar, g5, g5p, bsum, dh, gws, bias, gain = take(9)
    first_own, first_in, second_own, second_in = take(4)
    blocks, others, bias_blocks, bias_others = [None, *take(2)], [None, *take(2)], take(3), take(3)
    wres = next(names)
    local_sem, send_sem, recv_sem = take(3)

    pos, core, dp, seq = here()
    partner = place(pos, 1 - core)
    left, right = (dp, (seq + 7) & 7), (dp, (seq + 1) & 7)
    onward = {n: [place(moved(pos, a, (pos[a] + n) & 3), core) for a in range(3)] for n in (1, 2, 3)}
    beside = [[place(moved(pos, a, to(pos[a])), core) for a in range(3)] for to in (lambda c: c ^ 1, lambda c: 3 - c)]
    inside = (seq > 0, seq < 7)

    def remote(n, src, dst, device):
        return pltpu.make_async_remote_copy(
            src_ref=src, dst_ref=dst, send_sem=send_sem.at[n], recv_sem=recv_sem.at[n],
            device_id=device, device_id_type=MESH,
        )

    def local(n, src, dst):
        return pltpu.make_async_copy(src, dst, local_sem.at[n])

    in_bases = local(0, bases, bases_e.at[:, pl.ds(128, ROWS)])
    in_up = local(1, up, up_e.at[pl.ds(HALO, ROWS)])
    in_row = [local(2, bias_in, bias.at[0]), local(3, gain_in, gain.at[0])]
    in_w = [local(6 + p, weight.at[:, pl.ds(p * WIDE, WIDE)], w_v.at[:, pl.ds(p * WIDE, WIDE)]) for p in range(GROUPS)]
    in_cot = local(9, cot, cot_e.at[pl.ds(HALO, ROWS)])
    for copy in (in_bases, in_up, *in_row, *in_w, in_cot):
        copy.start()

    barrier = pltpu.get_barrier_semaphore()
    partners = [partner, left, right]
    partners += [device for devices in onward.values() for device in devices]
    for device in partners:
        pl.semaphore_signal(barrier, inc=1, device_id=device, device_id_type=MESH)

    halos = [
        remote(0, bases.at[:, pl.ds(ROWS - 128, 128)], bases_e.at[:, pl.ds(0, 128)], right),
        remote(1, bases.at[:, pl.ds(0, 128)], bases_e.at[:, pl.ds(128 + ROWS, 128)], left),
    ]
    for n, (source, target) in enumerate(((up, up_e), (cot, cot_e))):
        halos += [
            remote(2 + 2 * n, source.at[pl.ds(ROWS - HALO, HALO)], target.at[pl.ds(0, HALO)], right),
            remote(3 + 2 * n, source.at[pl.ds(0, HALO)], target.at[pl.ds(HALO + ROWS, HALO)], left),
        ]
    h_copy = remote(6, hs.at[1], h_in, partner)

    def g_copy(p):
        return remote(7 + p, gbuf.at[p], gpar.at[p], partner)

    row = lax.broadcasted_iota(jnp.int32, (HALF, 128), 0)
    column = lax.broadcasted_iota(jnp.int32, (HALF, 128), 1)
    sixth = (row * 10923) >> 16
    last = row - 6 * sixth
    first, second, third = sixth >> 4, (sixth >> 2) & 3, sixth & 3
    channel = (first >> 1) * 384 + second * 96 + third * 12 + (first & 1) * 6 + last
    for n, c in enumerate((core, 1 - core)):
        for b in range(C // 128):
            hit = column + b * 128 == channel + c * 48
            perm_v[n * HALF : (n + 1) * HALF, b * 128 : (b + 1) * 128] = hit.astype(F32).astype(BF)
    turned = second * 96 + third * 24 + first * 6 + last
    for b in range(HALF // 128):
        permz_v[:, b * 128 : (b + 1) * 128] = (column + b * 128 == turned).astype(F32).astype(BF)

    tab[...] = jnp.zeros(tab.shape, F32)
    tab[0:4, :] = table[...].astype(F32)
    bsum[...] = jnp.zeros(bsum.shape, F32)
    code = lax.broadcasted_iota(jnp.int32, (8, 128), 0)

    def embedded(block):
        onehot = (code == bases_e[:, pl.ds(times(block, 128), 128)]).astype(F32)
        return lax.dot_general(onehot, tab[...], TN, preferred_element_type=F32)

    def normed_of(x):
        r = lax.rsqrt(jnp.mean(x * x, axis=-1, keepdims=True) + 1e-06)
        return r, (x * r * gain[...])

    def norm_block(pair, carry):
        both = [embedded(2 * pair + 1), embedded(2 * pair + 2)]
        for s in range(8):
            row = pl.multiple_of(pair * 256 + s * 32, 32)
            x = up_e[pl.ds(row + HALO, 32), :].astype(F32) + both[s // 4][s % 4 * 32 : s % 4 * 32 + 32]
            r, h = normed_of(x)
            xs[pl.ds(row, 32), :] = x
            rin[pl.ds(row, 32), :] = jnp.broadcast_to(r, (32, 128))
            hb[pl.ds(row + 2 * HALO, 32), :] = h.astype(BF)
        return carry

    def norm():
        for copy in (in_bases, in_up, *in_row):
            copy.wait()
        lax.fori_loop(0, ROWS // 256, norm_block, 0)
        pl.semaphore_wait(barrier, len(partners))
        for copy in halos:
            copy.start()

    def norm_ends():
        for copy in halos:
            copy.wait_recv()
        hb[0:HALO, :] = jnp.zeros((HALO, C), BF)
        hb[HALO + EXT : 2 * HALO + EXT, :] = jnp.zeros((HALO, C), BF)
        for side, (block, skip) in enumerate(((0, 128 - HALO), (1 + ROWS // 128, 0))):
            start = side * (HALO + ROWS)
            x = up_e[start : start + HALO, :].astype(F32) + embedded(block)[skip : skip + HALO]
            h = jnp.where(inside[side], normed_of(x)[1], 0.0)
            hb[start + HALO : start + 2 * HALO, :] = h.astype(BF)

    def turn():
        for n in range(2):
            rows = perm_v[(1 - n) * HALF : (2 - n) * HALF, :]
            h_own = hb[2 * HALO : 2 * HALO + ROWS, :]
            hs[1 - n] = lax.dot_general(rows, h_own, NT, preferred_element_type=F32).astype(BF)
            if n == 0:
                h_copy.start()


    def shift_h():
        def tile(j, carry):
            row = times(j, 96)
            for p in range(GROUPS):
                v = hb[pl.ds(row, 128), p * WIDE : (p + 1) * WIDE].astype(F32)
                for k in range(TAPS):
                    h5[pl.ds(row, 96), k * C + p * WIDE : k * C + (p + 1) * WIDE] = v[8 + STEP * k : 104 + STEP * k].astype(BF)
            return carry

        lax.fori_loop(0, EXT // 96, tile, 0)

    c0 = np.float32(np.sqrt(2 / np.pi))

    def gelu_pair(z):
        square = z * z
        t = jnp.tanh(c0 * z * (1 + 0.044715 * square))
        cdf = 0.5 + 0.5 * t
        slope = cdf + (0.5 * c0) * z * (1 - t * t) * (1 + 0.134145 * square)
        return z * cdf, slope

    def forward(p):
        cols = pl.ds(times(p, WIDE), WIDE)
        for n in range(GROUPS):
            pl.when(p == n)(in_w[n].wait)
        pl.when(p == 0)(in_cot.wait)
        half = EXT // 2

        def tile(row, n):
            act, slope = gelu_pair(pre[row + HALO : row + HALO + n, :] + bias[:, cols])
            ob[row : row + n, cols] = (xs[row : row + n, cols] + act).astype(BF)
            gbuf[p, row + HALO : row + HALO + n, :] = (cot_e[row + HALO : row + HALO + n, cols].astype(F32) * slope).astype(BF)

        pre[0:half, :] = jnp.dot(h5[0:half, :], w_v[:, cols], preferred_element_type=F32)
        for row in range(0, half - HALO, 64):
            tile(row, 64)
        pre[half:, :] = jnp.dot(h5[half:, :], w_v[:, cols], preferred_element_type=F32)
        for row in range(half - HALO, ROWS, 64):
            tile(row, 64)
        for side in range(2):
            rows = slice(side * (HALO + ROWS), side * (HALO + ROWS) + HALO)
            _, slope = gelu_pair(pre[rows, :] + bias[:, cols])
            g = jnp.where(inside[side], cot_e[rows, cols].astype(F32) * slope, 0.0)
            gbuf[p, rows, :] = g.astype(BF)
        g_copy(p).start()

    def shift_g(source, p, target, column):
        def tile(j, total):
            row = times(j, 128)
            v = source[p, pl.ds(row, 160), :].astype(F32)
            for k in range(TAPS):
                target[pl.ds(row, 128), pl.ds(column(k), WIDE)] = v[24 - STEP * k : 152 - STEP * k].astype(BF)
            return total + jnp.sum(v[16:144].reshape(16, 8, WIDE), axis=0)

        bsum[:, pl.ds(times(p, WIDE), WIDE)] += lax.fori_loop(0, ROWS // 128, tile, jnp.zeros((8, WIDE), F32))

    def axis_of(kind, stage):
        return (kind, jnp.where(kind == 0, 1, 0), jnp.where(kind == 2, 1, 2))[stage]

    def pick_of(axis, three):
        return jnp.where(axis == 0, three[0], jnp.where(axis == 1, three[1], three[2]))

    def along(axis):
        return pick_of(axis, pos)

    def device_of(axis, three):
        return tuple(pick_of(axis, [device[n] for device in three]) for n in range(2))

    def kind_of(p, m):
        return jnp.where(p + m >= 3, p + m - 3, p + m)

    def step_sem(p, step):
        return 10 + 4 * p + step

    def step_wait(p, step):
        whole = (first_in, second_in, others[1], others[2])[step].at[p]
        return remote(step_sem(p, step), whole, whole, partner)

    def hops(n, axis, source, target):
        c = along(axis)
        return [
            remote(n, source((c + delta) & 3), target(delta - 1), device_of(axis, onward[delta])) for delta in (1, 2, 3)
        ]

    def kept_set(c, odd):
        return c >> 1 if odd else ((c + 1) >> 1) & 1

    def mine_of(c, odd):
        return c & 1 if odd else c >> 1

    def pair_copy(p, m, n, step):
        kind, slot, odd = kind_of(p, m), 2 * m + n, n
        c = along(kind)
        flip = (step == 0) == (odd == 0)
        other = device_of(kind, beside[0 if flip else 1])
        if step == 0:
            to = c ^ 1 if flip else 3 - c
            source = first_own.at[p, slot, pl.ds(2 * kept_set(to, odd), 2)]
            return remote(step_sem(p, step), source, first_in.at[p, slot], other)
        return remote(step_sem(p, step), second_own.at[p, slot], second_in.at[p, slot], other)

    def piece_hops(p, m, stage):
        slot, count = SLOTS[m]
        return hops(
            step_sem(p, stage + 1),
            axis_of(kind_of(p, m), stage),
            lambda d: blocks[stage].at[p, d, pl.ds(slot, count)],
            lambda d: others[stage].at[p, d, pl.ds(slot, count)],
        )

    def bias_hops(stage):
        return hops(
            22 + stage,
            jnp.int32(stage),
            lambda d: bias_blocks[stage].at[d],
            lambda d: bias_others[stage].at[d],
        )

    def bias_wait(stage):
        return remote(22 + stage, bias_others[stage], bias_others[stage], partner)

    def weights(p):
        shift_g(gbuf, p, g5, lambda k: pl.multiple_of(k * C + p * WIDE, WIDE))
        g_copy(p).wait_recv()
        shift_g(gpar, p, g5p, lambda k: TAP_OF.index(k) * WIDE)

        @pl.when(p == 0)
        def _():
            h_copy.wait_recv()

        def piece(m, first, count):
            own = [g5[:, pl.ds(pl.multiple_of(lax.rem(3 * (first + n), TAPS) * C + p * WIDE, WIDE), WIDE)] for n in range(count)]
            other = g5p[:, pl.ds(times(first, WIDE), count * WIDE)]
            rhs = jnp.concatenate([jnp.concatenate(own, axis=1) if count > 1 else own[0], other], axis=0)
            lhs = jnp.concatenate([hs[0], h_in[...]], axis=1)
            wres[:, 0 : count * WIDE] = jnp.dot(lhs, rhs, preferred_element_type=F32)
            kind = kind_of(p, m)
            wide = count * WIDE

            def store(block):
                for d in range(4):
                    rows = block(d).astype(BF)
                    for n in range(count):
                        first_own[p, first + n, KEPT[n][d]] = rows[:, n * WIDE : (n + 1) * WIDE]

            @pl.when(kind == 0)
            def _():
                store(lambda d: wres[d * 96 : d * 96 + 96, 0:wide])

            @pl.when(kind == 1)
            def _():
                store(lambda d: jnp.concatenate([wres[e * 96 + d * 24 : e * 96 + d * 24 + 24, 0:wide] for e in range(4)], axis=0))

            @pl.when(kind == 2)
            def _():
                r = jnp.dot(permz_v[...], wres[:, 0:wide].astype(BF), preferred_element_type=F32)
                store(lambda d: r[d * 96 : d * 96 + 96])

            for n in range(count):
                pair_copy(p, m, n, 0).start()

        def pair(m, carry):
            piece(m, 2 * m, 2)
            return carry

        lax.fori_loop(0, 2, pair, 0)
        piece(2, 4, 1)

        @pl.when(p == GROUPS - 1)
        def _():
            total = jnp.sum(bsum[...], axis=0, keepdims=True)
            total = jnp.broadcast_to(total, (128, C)).astype(BF)
            r = lax.dot_general(perm_v[0:HALF, :], total, NT, preferred_element_type=F32)
            for d in range(4):
                bias_blocks[0][d] = r[d * 96 : d * 96 + 96].astype(BF)
            for copy in bias_hops(0):
                copy.start()

    def spread_of(shape, sixteenth):
        r, c = lax.broadcasted_iota(jnp.int32, shape, 0), lax.broadcasted_iota(jnp.int32, shape, 1)
        return sixteenth(c, 6 * (r >> 4), r & 15).astype(F32).astype(BF)

    spread = spread_of((64, 32), lambda c, base, w: (w < 6) & (c == base + w))
    spread_two = spread_of((64, 48), lambda c, base, w: ((w & 7) < 6) & (c == base + (w & 7) + 24 * (w >> 3)))

    def handed_on(total, stage, store):
        if stage == 0:
            for d in range(4):
                block = jnp.concatenate([total[24 * d : 24 * d + 24], jnp.zeros((8, total.shape[1]), F32)], axis=0)
                store(d, block.astype(BF))
        else:
            r = jnp.dot(spread, total.astype(BF), preferred_element_type=F32).astype(BF)
            for d in range(4):
                store(d, r[16 * d : 16 * d + 16])

    def finish_first(p, step):
        step_wait(p, step).wait_recv()
        for m, (first, count) in enumerate(SLOTS):
            c = along(kind_of(p, m))
            for slot in range(first, first + count):
                odd = slot % 2
                mine = mine_of(c, odd)
                if step == 0:
                    mine = 1 - mine
                total = first_own[p, slot, 2 * kept_set(c, odd) + mine].astype(F32) + first_in[p, slot, mine].astype(F32)
                if step == 0:
                    second_own[p, slot, 0] = total.astype(BF)
                    pair_copy(p, m, odd, 1).start()
                else:
                    total = total + second_in[p, slot, 0].astype(F32)
                    for d in range(4):
                        rows = total[24 * d : 24 * d + 24]
                        block = jnp.concatenate([rows[:, 0:128], rows[:, 128:]], axis=0)
                        blocks[1][p, d, slot] = block.astype(BF)
            if step == 1:
                for copy in piece_hops(p, m, 1):
                    copy.start()

    def finish_next(p, stage):
        step_wait(p, stage + 1).wait_recv()
        for m, (first, count) in enumerate(SLOTS):
            own = along(axis_of(kind_of(p, m), stage))
            for slot in range(first, first + count):
                total = blocks[stage][p, own, slot].astype(F32)
                for d in range(3):
                    total = total + others[stage][p, d, slot].astype(F32)
                if stage == 1:
                    r = jnp.dot(spread_two, total.astype(BF), preferred_element_type=F32).astype(BF)
                    for d in range(4):
                        blocks[2][p, d, slot] = r[16 * d : 16 * d + 16]
                else:
                    for half in range(2):
                        gws[TAP_OF[slot], :, pl.ds(times(2 * p + half, 128), 128)] = total[8 * half : 8 * half + 8]
            if stage == 1:
                for copy in piece_hops(p, m, 2):
                    copy.start()

    def finish(p, step):
        if step < 2:
            finish_first(p, step)
        else:
            finish_next(p, step - 1)

    def finish_bias(stage):
        bias_wait(stage).wait_recv()
        total = bias_blocks[stage][pos[stage]].astype(F32)
        for d in range(3):
            total = total + bias_others[stage][d].astype(F32)
        if stage == 2:
            gws[TAPS, :, 0:128] = total[0:8]
        else:

            def store(d, value):
                bias_blocks[stage + 1][d] = value

            handed_on(total, stage, store)
            for copy in bias_hops(stage + 1):
                copy.start()

    def hidden(t):
        rows = pl.ds(times(t, TILE), TILE)
        return sum(
            lax.dot_general(g5[rows, k * C : (k + 1) * C], w_v[k * C : (k + 1) * C, :], NT, preferred_element_type=F32)
            for k in range(TAPS)
        )

    def input_gradient(t):
        for i in range(TILE // 32):
            row = pl.multiple_of(t * TILE + i * 32, 32)
            r = jnp.concatenate([rin[pl.ds(row, 32), :]] * (C // 128), axis=1)
            normed = xs[pl.ds(row, 32), :] * r
            dn = dh[i * 32 : i * 32 + 32, :] * gain[...]
            mean = jnp.mean(dn * normed, axis=-1, keepdims=True)
            g = cot_e[pl.ds(row + HALO, 32), :].astype(F32) + (dn - normed * mean) * r
            gi[pl.ds(row, 32), :] = g.astype(BF)

    def backward(t):
        input_gradient(jnp.maximum(t - 1, 0))
        dh[...] = hidden(t)

    def during(s, start, stop, step):
        if stop > start:
            pl.when((s >= start) & (s < stop))(step)

    def turn_of(s, carry):
        during(s, 0, 3, lambda: forward(s))
        during(s, 1, 4, lambda: weights(s - 1))
        during(s, 4, 8, lambda: backward(s - 4))
        for step in range(4):
            during(s, 2 + step, 5 + step, lambda: finish(s - 2 - step, step))
            if step < 3:
                during(s, 5 + step, 6 + step, lambda: finish_bias(step))
        return carry

    norm()
    turn()
    norm_ends()
    shift_h()
    dh[...] = jnp.zeros(dh.shape, F32)
    lax.fori_loop(0, 8, turn_of, 0)
    input_gradient(ROWS // TILE - 1)

    gw[...] = gws[0:TAPS, 0:6, :]
    mine = (dp * 8 + seq) * 6
    base = jnp.minimum((mine >> 4) * 16, C - 32)
    pick_row = lax.broadcasted_iota(jnp.int32, (8, 32), 0)
    pick_col = lax.broadcasted_iota(jnp.int32, (8, 32), 1)
    pick = (pick_col == pick_row + (mine - base)).astype(F32).astype(BF)
    total = jnp.zeros((8, C), F32)
    for k in range(TAPS):
        rows = w_v[pl.ds(pl.multiple_of(k * C + base, 16), 32), :]
        total = total + jnp.dot(pick, rows, preferred_element_type=F32) * gws[k]
    lane = lax.broadcasted_iota(jnp.int32, (8, C), 1)
    row = lax.broadcasted_iota(jnp.int32, (8, C), 0)
    own_gain = jnp.sum(jnp.where(lane == row + mine, gain[...], 0.0), axis=-1, keepdims=True)
    column = jnp.sum(total, axis=-1, keepdims=True) / own_gain
    diagonal = (lane == row)[:, 0:128] & (row < 6)[:, 0:128]
    small[0:1, :] = jnp.sum(jnp.where(diagonal, gws[TAPS, :, 0:128], 0.0), axis=0, keepdims=True)
    small[1:2, :] = jnp.sum(jnp.where(diagonal, column, 0.0), axis=0, keepdims=True)

    for copy in (*halos, h_copy):
        copy.wait_send()
    for stage in range(STAGES):
        bias_wait(stage).wait_send()

    def sent(p, carry):
        g_copy(p).wait_send()
        for step in range(4):
            step_wait(p, step).wait_send()
        return carry

    lax.fori_loop(0, GROUPS, sent, 0)


MESH = pl.DeviceIdType.MESH


def body(bases, upsampled, base_table, filter_weight, filter_bias, norm_gain, cotangent):
    vmem, hbm = pl.BlockSpec(memory_space=pltpu.VMEM), pl.BlockSpec(memory_space=pl.ANY)
    scratch = [
        pltpu.VMEM((1, ROWS + 256), jnp.int32),
        pltpu.VMEM((EXT, C), BF),
        pltpu.VMEM((EXT, C), BF),
        pltpu.VMEM((TAPS * C, C), BF),
        pltpu.VMEM((C, C), BF),
        pltpu.VMEM((HALF, HALF), BF),
        pltpu.VMEM((8, C), F32),
        pltpu.VMEM((ROWS, C), F32),
        pltpu.VMEM((ROWS, 128), F32),
        pltpu.VMEM((EXT + 2 * HALO, C), BF),
        pltpu.VMEM((EXT, TAPS * C), BF),
        pltpu.VMEM((2, HALF, ROWS), BF),
        pltpu.VMEM((HALF, ROWS), BF),
        pltpu.VMEM((EXT, WIDE), F32),
        pltpu.VMEM((GROUPS, EXT, WIDE), BF),
        pltpu.VMEM((GROUPS, EXT, WIDE), BF),
        pltpu.VMEM((ROWS, TAPS * C), BF),
        pltpu.VMEM((ROWS, TAPS * WIDE), BF),
        pltpu.VMEM((8, C), F32),
        pltpu.VMEM((TILE, C), F32),
        pltpu.VMEM((TAPS + 1, 8, C), F32),
        pltpu.VMEM((1, C), F32),
        pltpu.VMEM((1, C), F32),
    ]
    scratch += [pltpu.VMEM((GROUPS, TAPS, n, 96, WIDE), BF) for n in (4, 2, 1, 1)]
    scratch += [pltpu.VMEM((GROUPS, 4, TAPS, rows, 128), BF) for rows in (48, 16)]
    scratch += [pltpu.VMEM((GROUPS, 3, TAPS, rows, 128), BF) for rows in (48, 16)]
    scratch += [pltpu.VMEM((4, rows, 128), BF) for rows in BLOCK_ROWS]
    scratch += [pltpu.VMEM((3, rows, 128), BF) for rows in BLOCK_ROWS]
    scratch += [pltpu.VMEM((HALF, 2 * WIDE), F32)]
    remotes = 10 + 4 * GROUPS + STAGES
    scratch += [
        pltpu.SemaphoreType.DMA((16,)),
        pltpu.SemaphoreType.DMA((remotes,)),
        pltpu.SemaphoreType.DMA((remotes,)),
    ]
    out, gin, gw, small = pl.pallas_call(
        kernel,
        out_shape=[
            pltpu.VMEM((ROWS, C), BF),
            pltpu.VMEM((ROWS, C), BF),
            pltpu.VMEM((TAPS, 6, C), F32),
            pltpu.VMEM((8, 128), F32),
        ],
        in_specs=[hbm, hbm, vmem, hbm, hbm, hbm, hbm],
        out_specs=[vmem, vmem, vmem, vmem],
        scratch_shapes=scratch,
        compiler_params=pltpu.CompilerParams(collective_id=0, has_side_effects=True, vmem_limit_bytes=58 * 2**20),
        name="block",
    )(
        bases,
        upsampled[0],
        base_table,
        filter_weight.reshape(TAPS * C, C),
        filter_bias,
        norm_gain,
        cotangent[0],
    )
    return out[None], gin[None], gw, small[0, 0:6], small[1, 0:6]


def solution(mesh):
    placed = (P("dp", "seq"), P("dp", "seq", None), P(), P(), P(), P(), P("dp", "seq", None))
    return jax.shard_map(
        body,
        mesh=mesh,
        in_specs=placed,
        out_specs=(
            P("dp", "seq", None),
            P("dp", "seq", None),
            P(None, ("dp", "seq"), None),
            P(("dp", "seq")),
            P(("dp", "seq")),
        ),
        check_vma=False,
    )
```

```python
import jax
import jax.numpy as jnp
import numpy as np
from jax import lax
from jax.experimental import pallas as pl
from jax.experimental.pallas import tpu as pltpu
from jax.sharding import PartitionSpec as P

BF, F32 = jnp.bfloat16, jnp.float32
C, TAPS, STEP = 768, 5, 4
ROWS, HALO = 1024, 16
EXT = ROWS + 2 * HALO
WIDE = 256
GROUPS = C // WIDE
HALF = C // 2
NT = (((1,), (1,)), ((), ()))
TN = (((0,), (0,)), ((), ()))

TAP_OF = [3 * slot % TAPS for slot in range(TAPS)]
SLOTS = ((0, 2), (2, 2), (4, 1))
STAGES = 3
KEPT = ((0, 2, 3, 1), (0, 1, 2, 3))
TILE = 256
BLOCK_ROWS = (96, 32, 16)


def here():
    dp, seq = lax.axis_index("dp"), lax.axis_index("seq")
    return [2 * (dp >> 3) + (seq & 1), (dp >> 1) & 3, seq >> 1], dp & 1, dp, seq


def place(pos, core):
    x, y, z = pos
    return ((x >> 1) * 8 + y * 2 + core, z * 2 + (x & 1))


def moved(pos, axis, to):
    other = list(pos)
    other[axis] = to
    return other


def times(value, step):
    return pl.multiple_of(value * step, step)


def kernel(*refs):
    names = iter(refs)

    def take(n):
        return [next(names) for _ in range(n)]

    bases, up, table, weight, bias_in, gain_in, cot = take(7)
    ob, gi, gw, small = take(4)
    bases_e, up_e, cot_e, w_v, perm_v, permz_v, tab, xs, rin, hb, h5, hs, h_in, pre = take(14)
    gbuf, gpar, g5, g5p, bsum, dh, gws, bias, gain = take(9)
    first_own, first_in, second_own, second_in = take(4)
    blocks, others, bias_blocks, bias_others = [None, *take(2)], [None, *take(2)], take(3), take(3)
    wres, mid, swap_v = take(3)
    local_sem, send_sem, recv_sem = take(3)

    pos, core, dp, seq = here()
    partner = place(pos, 1 - core)
    left, right = (dp, (seq + 7) & 7), (dp, (seq + 1) & 7)
    onward = {n: [place(moved(pos, a, (pos[a] + n) & 3), core) for a in range(3)] for n in (1, 2, 3)}
    beside = [[place(moved(pos, a, to(pos[a])), core) for a in range(3)] for to in (lambda c: c ^ 1, lambda c: 3 - c)]
    inside = (seq > 0, seq < 7)

    def remote(n, src, dst, device):
        return pltpu.make_async_remote_copy(
            src_ref=src, dst_ref=dst, send_sem=send_sem.at[n], recv_sem=recv_sem.at[n],
            device_id=device, device_id_type=MESH,
        )

    def local(n, src, dst):
        return pltpu.make_async_copy(src, dst, local_sem.at[n])

    in_bases = local(0, bases, bases_e.at[:, pl.ds(128, ROWS)])
    in_up = local(1, up, up_e.at[pl.ds(HALO, ROWS)])
    in_row = [local(2, bias_in, bias.at[0]), local(3, gain_in, gain.at[0])]
    in_w = [local(6 + p, weight.at[:, pl.ds(p * WIDE, WIDE)], w_v.at[:, pl.ds(p * WIDE, WIDE)]) for p in range(GROUPS)]
    in_cot = local(9, cot, cot_e.at[pl.ds(HALO, ROWS)])
    for copy in (in_bases, in_up, *in_row, *in_w, in_cot):
        copy.start()

    barrier = pltpu.get_barrier_semaphore()
    partners = [partner, left, right]
    partners += [device for devices in onward.values() for device in devices]
    for device in partners:
        pl.semaphore_signal(barrier, inc=1, device_id=device, device_id_type=MESH)

    halos = [
        remote(0, bases.at[:, pl.ds(ROWS - 128, 128)], bases_e.at[:, pl.ds(0, 128)], right),
        remote(1, bases.at[:, pl.ds(0, 128)], bases_e.at[:, pl.ds(128 + ROWS, 128)], left),
    ]
    for n, (source, target) in enumerate(((up, up_e), (cot, cot_e))):
        halos += [
            remote(2 + 2 * n, source.at[pl.ds(ROWS - HALO, HALO)], target.at[pl.ds(0, HALO)], right),
            remote(3 + 2 * n, source.at[pl.ds(0, HALO)], target.at[pl.ds(HALO + ROWS, HALO)], left),
        ]
    h_copy = remote(6, hs.at[1], h_in, partner)

    def g_copy(p):
        return remote(7 + p, gbuf.at[p], gpar.at[p], partner)

    row = lax.broadcasted_iota(jnp.int32, (HALF, 128), 0)
    column = lax.broadcasted_iota(jnp.int32, (HALF, 128), 1)
    sixth = (row * 10923) >> 16
    last = row - 6 * sixth
    first, second, third = sixth >> 4, (sixth >> 2) & 3, sixth & 3
    channel = (first >> 1) * 384 + second * 96 + third * 12 + (first & 1) * 6 + last
    for n, c in enumerate((core, 1 - core)):
        for b in range(C // 128):
            hit = column + b * 128 == channel + c * 48
            perm_v[n * HALF : (n + 1) * HALF, b * 128 : (b + 1) * 128] = hit.astype(F32).astype(BF)
    turned = second * 96 + third * 24 + first * 6 + last
    for b in range(HALF // 128):
        permz_v[:, b * 128 : (b + 1) * 128] = (column + b * 128 == turned).astype(F32).astype(BF)

    swapped = ((sixth & 3) * 24 + ((sixth >> 2) & 3) * 6 + last)[0:96]
    swap_v[...] = (column[0:96] == swapped).astype(F32).astype(BF)

    tab[...] = jnp.zeros(tab.shape, F32)
    mid[...] = jnp.zeros(mid.shape, F32)
    tab[0:4, :] = table[...].astype(F32)
    bsum[...] = jnp.zeros(bsum.shape, F32)
    code = lax.broadcasted_iota(jnp.int32, (8, 128), 0)

    def embedded(block):
        onehot = (code == bases_e[:, pl.ds(times(block, 128), 128)]).astype(F32)
        return lax.dot_general(onehot, tab[...], TN, preferred_element_type=F32)

    def normed_of(x):
        r = lax.rsqrt(jnp.mean(x * x, axis=-1, keepdims=True) + 1e-06)
        return r, (x * r * gain[...])

    def norm_block(pair, carry):
        both = [embedded(2 * pair + 1), embedded(2 * pair + 2)]
        for s in range(8):
            row = pl.multiple_of(pair * 256 + s * 32, 32)
            x = up_e[pl.ds(row + HALO, 32), :].astype(F32) + both[s // 4][s % 4 * 32 : s % 4 * 32 + 32]
            r, h = normed_of(x)
            xs[pl.ds(row, 32), :] = x
            rin[pl.ds(row, 32), :] = jnp.broadcast_to(r, (32, 128))
            hb[pl.ds(row + 2 * HALO, 32), :] = h.astype(BF)
        return carry

    def norm():
        for copy in (in_bases, in_up, *in_row):
            copy.wait()
        lax.fori_loop(0, ROWS // 256, norm_block, 0)
        pl.semaphore_wait(barrier, len(partners))
        for copy in halos:
            copy.start()

    def norm_ends():
        for copy in halos:
            copy.wait_recv()
        hb[0:HALO, :] = jnp.zeros((HALO, C), BF)
        hb[HALO + EXT : 2 * HALO + EXT, :] = jnp.zeros((HALO, C), BF)
        for side, (block, skip) in enumerate(((0, 128 - HALO), (1 + ROWS // 128, 0))):
            start = side * (HALO + ROWS)
            x = up_e[start : start + HALO, :].astype(F32) + embedded(block)[skip : skip + HALO]
            h = jnp.where(inside[side], normed_of(x)[1], 0.0)
            hb[start + HALO : start + 2 * HALO, :] = h.astype(BF)

    def turn():
        for n in range(2):
            rows = perm_v[(1 - n) * HALF : (2 - n) * HALF, :]
            h_own = hb[2 * HALO : 2 * HALO + ROWS, :]
            hs[1 - n] = lax.dot_general(rows, h_own, NT, preferred_element_type=F32).astype(BF)
            if n == 0:
                h_copy.start()


    def shift_h():
        def tile(j, carry):
            row = times(j, 96)
            for p in range(GROUPS):
                v = hb[pl.ds(row, 128), p * WIDE : (p + 1) * WIDE].astype(F32)
                for k in range(TAPS):
                    h5[pl.ds(row, 96), k * C + p * WIDE : k * C + (p + 1) * WIDE] = v[8 + STEP * k : 104 + STEP * k].astype(BF)
            return carry

        lax.fori_loop(0, EXT // 96, tile, 0)

    c0 = np.float32(np.sqrt(2 / np.pi))

    def gelu_pair(z):
        square = z * z
        t = jnp.tanh(c0 * z * (1 + 0.044715 * square))
        cdf = 0.5 + 0.5 * t
        slope = cdf + (0.5 * c0) * z * (1 - t * t) * (1 + 0.134145 * square)
        return z * cdf, slope

    def forward(p):
        cols = pl.ds(times(p, WIDE), WIDE)
        for n in range(GROUPS):
            pl.when(p == n)(in_w[n].wait)
        pl.when(p == 0)(in_cot.wait)
        half = EXT // 2

        def tile(row, n):
            act, slope = gelu_pair(pre[row + HALO : row + HALO + n, :] + bias[:, cols])
            ob[row : row + n, cols] = (xs[row : row + n, cols] + act).astype(BF)
            gbuf[p, row + HALO : row + HALO + n, :] = (cot_e[row + HALO : row + HALO + n, cols].astype(F32) * slope).astype(BF)

        pre[0:half, :] = jnp.dot(h5[0:half, :], w_v[:, cols], preferred_element_type=F32)
        for row in range(0, half - HALO, 64):
            tile(row, 64)
        pre[half:, :] = jnp.dot(h5[half:, :], w_v[:, cols], preferred_element_type=F32)
        for row in range(half - HALO, ROWS, 64):
            tile(row, 64)
        for side in range(2):
            rows = slice(side * (HALO + ROWS), side * (HALO + ROWS) + HALO)
            _, slope = gelu_pair(pre[rows, :] + bias[:, cols])
            g = jnp.where(inside[side], cot_e[rows, cols].astype(F32) * slope, 0.0)
            gbuf[p, rows, :] = g.astype(BF)
        g_copy(p).start()

    def shift_g(source, p, target, column):
        def tile(j, total):
            row = times(j, 128)
            v = source[p, pl.ds(row, 160), :].astype(F32)
            for k in range(TAPS):
                target[pl.ds(row, 128), pl.ds(column(k), WIDE)] = v[24 - STEP * k : 152 - STEP * k].astype(BF)
            return total + jnp.sum(v[16:144].reshape(16, 8, WIDE), axis=0)

        bsum[:, pl.ds(times(p, WIDE), WIDE)] += lax.fori_loop(0, ROWS // 128, tile, jnp.zeros((8, WIDE), F32))

    def axis_of(kind, stage):
        return jnp.where(kind + stage >= 3, kind + stage - 3, kind + stage)

    def pick_of(axis, three):
        return jnp.where(axis == 0, three[0], jnp.where(axis == 1, three[1], three[2]))

    def along(axis):
        return pick_of(axis, pos)

    def device_of(axis, three):
        return tuple(pick_of(axis, [device[n] for device in three]) for n in range(2))

    def kind_of(p, m):
        return jnp.where(p + m >= 3, p + m - 3, p + m)

    def step_sem(p, step):
        return 10 + 4 * p + step

    def step_wait(p, step):
        whole = (first_in, second_in, others[1], others[2])[step].at[p]
        return remote(step_sem(p, step), whole, whole, partner)

    def hops(n, axis, source, target):
        c = along(axis)
        return [
            remote(n, source((c + delta) & 3), target(delta - 1), device_of(axis, onward[delta])) for delta in (1, 2, 3)
        ]

    def kept_set(c, odd):
        return c >> 1 if odd else ((c + 1) >> 1) & 1

    def mine_of(c, odd):
        return c & 1 if odd else c >> 1

    def pair_copy(p, m, n, step):
        kind, slot, odd = kind_of(p, m), 2 * m + n, n
        c = along(kind)
        flip = (step == 0) == (odd == 0)
        other = device_of(kind, beside[0 if flip else 1])
        if step == 0:
            to = c ^ 1 if flip else 3 - c
            source = first_own.at[p, slot, pl.ds(2 * kept_set(to, odd), 2)]
            return remote(step_sem(p, step), source, first_in.at[p, slot], other)
        return remote(step_sem(p, step), second_own.at[p, slot], second_in.at[p, slot], other)

    def piece_hops(p, m, stage):
        slot, count = SLOTS[m]
        return hops(
            step_sem(p, stage + 1),
            axis_of(kind_of(p, m), stage),
            lambda d: blocks[stage].at[p, d, pl.ds(slot, count)],
            lambda d: others[stage].at[p, d, pl.ds(slot, count)],
        )

    def bias_hops(stage):
        return hops(
            22 + stage,
            jnp.int32(stage),
            lambda d: bias_blocks[stage].at[d],
            lambda d: bias_others[stage].at[d],
        )

    def bias_wait(stage):
        return remote(22 + stage, bias_others[stage], bias_others[stage], partner)

    def weights(p):
        shift_g(gbuf, p, g5, lambda k: pl.multiple_of(k * C + p * WIDE, WIDE))
        g_copy(p).wait_recv()
        shift_g(gpar, p, g5p, lambda k: TAP_OF.index(k) * WIDE)

        @pl.when(p == 0)
        def _():
            h_copy.wait_recv()

        def piece(m, first, count):
            own = [g5[:, pl.ds(pl.multiple_of(lax.rem(3 * (first + n), TAPS) * C + p * WIDE, WIDE), WIDE)] for n in range(count)]
            other = g5p[:, pl.ds(times(first, WIDE), count * WIDE)]
            rhs = jnp.concatenate([jnp.concatenate(own, axis=1) if count > 1 else own[0], other], axis=0)
            lhs = jnp.concatenate([hs[0], h_in[...]], axis=1)
            wres[:, 0 : count * WIDE] = jnp.dot(lhs, rhs, preferred_element_type=F32)
            kind = kind_of(p, m)
            wide = count * WIDE

            def store(block):
                for d in range(4):
                    rows = block(d).astype(BF)
                    for n in range(count):
                        first_own[p, first + n, KEPT[n][d]] = rows[:, n * WIDE : (n + 1) * WIDE]

            @pl.when(kind == 0)
            def _():
                store(lambda d: wres[d * 96 : d * 96 + 96, 0:wide])

            @pl.when(kind == 1)
            def _():
                store(lambda d: jnp.concatenate([wres[e * 96 + d * 24 : e * 96 + d * 24 + 24, 0:wide] for e in range(4)], axis=0))

            @pl.when(kind == 2)
            def _():
                r = jnp.dot(permz_v[...], wres[:, 0:wide].astype(BF), preferred_element_type=F32)
                store(lambda d: r[d * 96 : d * 96 + 96])

            for n in range(count):
                pair_copy(p, m, n, 0).start()

        def pair(m, carry):
            piece(m, 2 * m, 2)
            return carry

        lax.fori_loop(0, 2, pair, 0)
        piece(2, 4, 1)

        @pl.when(p == GROUPS - 1)
        def _():
            total = jnp.sum(bsum[...], axis=0, keepdims=True)
            total = jnp.broadcast_to(total, (128, C)).astype(BF)
            r = lax.dot_general(perm_v[0:HALF, :], total, NT, preferred_element_type=F32)
            for d in range(4):
                bias_blocks[0][d] = r[d * 96 : d * 96 + 96].astype(BF)
            for copy in bias_hops(0):
                copy.start()

    def spread_of(shape, sixteenth):
        r, c = lax.broadcasted_iota(jnp.int32, shape, 0), lax.broadcasted_iota(jnp.int32, shape, 1)
        return sixteenth(c, 6 * (r >> 4), r & 15).astype(F32).astype(BF)

    spread = spread_of((64, 32), lambda c, base, w: (w < 6) & (c == base + w))
    spread_two = spread_of((64, 48), lambda c, base, w: ((w & 7) < 6) & (c == base + (w & 7) + 24 * (w >> 3)))

    def handed_on(total, stage, store):
        if stage == 0:
            for d in range(4):
                block = jnp.concatenate([total[24 * d : 24 * d + 24], jnp.zeros((8, total.shape[1]), F32)], axis=0)
                store(d, block.astype(BF))
        else:
            r = jnp.dot(spread, total.astype(BF), preferred_element_type=F32).astype(BF)
            for d in range(4):
                store(d, r[16 * d : 16 * d + 16])

    def finish_first(p, step):
        step_wait(p, step).wait_recv()
        for m, (first, count) in enumerate(SLOTS):
            c = along(kind_of(p, m))
            for slot in range(first, first + count):
                odd = slot % 2
                mine = mine_of(c, odd)
                if step == 0:
                    mine = 1 - mine
                total = first_own[p, slot, 2 * kept_set(c, odd) + mine].astype(F32) + first_in[p, slot, mine].astype(F32)
                if step == 0:
                    second_own[p, slot, 0] = total.astype(BF)
                    pair_copy(p, m, odd, 1).start()
                else:
                    mid[0:96, :] = total + second_in[p, slot, 0].astype(F32)

                    @pl.when(kind_of(p, m) == 1)
                    def _():
                        mid[0:96, :] = jnp.dot(swap_v[...], mid[...].astype(BF), preferred_element_type=F32)

                    for d in range(4):
                        rows = mid[24 * d : 24 * d + 24, :]
                        block = jnp.concatenate([rows[:, 0:128], rows[:, 128:]], axis=0)
                        blocks[1][p, d, slot] = block.astype(BF)
            if step == 1:
                for copy in piece_hops(p, m, 1):
                    copy.start()

    def finish_next(p, stage):
        step_wait(p, stage + 1).wait_recv()
        for m, (first, count) in enumerate(SLOTS):
            own = along(axis_of(kind_of(p, m), stage))
            for slot in range(first, first + count):
                total = blocks[stage][p, own, slot].astype(F32)
                for d in range(3):
                    total = total + others[stage][p, d, slot].astype(F32)
                if stage == 1:
                    r = jnp.dot(spread_two, total.astype(BF), preferred_element_type=F32).astype(BF)
                    for d in range(4):
                        blocks[2][p, d, slot] = r[16 * d : 16 * d + 16]
                else:
                    for half in range(2):
                        gws[TAP_OF[slot], :, pl.ds(times(2 * p + half, 128), 128)] = total[8 * half : 8 * half + 8]
            if stage == 1:
                for copy in piece_hops(p, m, 2):
                    copy.start()

    def finish(p, step):
        if step < 2:
            finish_first(p, step)
        else:
            finish_next(p, step - 1)

    def finish_bias(stage):
        bias_wait(stage).wait_recv()
        total = bias_blocks[stage][pos[stage]].astype(F32)
        for d in range(3):
            total = total + bias_others[stage][d].astype(F32)
        if stage == 2:
            gws[TAPS, :, 0:128] = total[0:8]
        else:

            def store(d, value):
                bias_blocks[stage + 1][d] = value

            handed_on(total, stage, store)
            for copy in bias_hops(stage + 1):
                copy.start()

    def hidden(t):
        rows = pl.ds(times(t, TILE), TILE)
        return sum(
            lax.dot_general(g5[rows, k * C : (k + 1) * C], w_v[k * C : (k + 1) * C, :], NT, preferred_element_type=F32)
            for k in range(TAPS)
        )

    def input_gradient(t):
        for i in range(TILE // 32):
            row = pl.multiple_of(t * TILE + i * 32, 32)
            r = jnp.concatenate([rin[pl.ds(row, 32), :]] * (C // 128), axis=1)
            normed = xs[pl.ds(row, 32), :] * r
            dn = dh[i * 32 : i * 32 + 32, :] * gain[...]
            mean = jnp.mean(dn * normed, axis=-1, keepdims=True)
            g = cot_e[pl.ds(row + HALO, 32), :].astype(F32) + (dn - normed * mean) * r
            gi[pl.ds(row, 32), :] = g.astype(BF)

    def backward(t):
        input_gradient(jnp.maximum(t - 1, 0))
        dh[...] = hidden(t)

    def during(s, start, stop, step):
        if stop > start:
            pl.when((s >= start) & (s < stop))(step)

    def turn_of(s, carry):
        during(s, 0, 3, lambda: forward(s))
        during(s, 1, 4, lambda: weights(s - 1))
        during(s, 4, 8, lambda: backward(s - 4))
        for step in range(4):
            during(s, 2 + step, 5 + step, lambda: finish(s - 2 - step, step))
            if step < 3:
                during(s, 5 + step, 6 + step, lambda: finish_bias(step))
        return carry

    norm()
    turn()
    norm_ends()
    shift_h()
    dh[...] = jnp.zeros(dh.shape, F32)
    lax.fori_loop(0, 8, turn_of, 0)
    input_gradient(ROWS // TILE - 1)

    gw[...] = gws[0:TAPS, 0:6, :]
    mine = (dp * 8 + seq) * 6
    base = jnp.minimum((mine >> 4) * 16, C - 32)
    pick_row = lax.broadcasted_iota(jnp.int32, (8, 32), 0)
    pick_col = lax.broadcasted_iota(jnp.int32, (8, 32), 1)
    pick = (pick_col == pick_row + (mine - base)).astype(F32).astype(BF)
    total = jnp.zeros((8, C), F32)
    for k in range(TAPS):
        rows = w_v[pl.ds(pl.multiple_of(k * C + base, 16), 32), :]
        total = total + jnp.dot(pick, rows, preferred_element_type=F32) * gws[k]
    lane = lax.broadcasted_iota(jnp.int32, (8, C), 1)
    row = lax.broadcasted_iota(jnp.int32, (8, C), 0)
    own_gain = jnp.sum(jnp.where(lane == row + mine, gain[...], 0.0), axis=-1, keepdims=True)
    column = jnp.sum(total, axis=-1, keepdims=True) / own_gain
    diagonal = (lane == row)[:, 0:128] & (row < 6)[:, 0:128]
    small[0:1, :] = jnp.sum(jnp.where(diagonal, gws[TAPS, :, 0:128], 0.0), axis=0, keepdims=True)
    small[1:2, :] = jnp.sum(jnp.where(diagonal, column, 0.0), axis=0, keepdims=True)

    for copy in (*halos, h_copy):
        copy.wait_send()
    for stage in range(STAGES):
        bias_wait(stage).wait_send()

    def sent(p, carry):
        g_copy(p).wait_send()
        for step in range(4):
            step_wait(p, step).wait_send()
        return carry

    lax.fori_loop(0, GROUPS, sent, 0)


MESH = pl.DeviceIdType.MESH


def body(bases, upsampled, base_table, filter_weight, filter_bias, norm_gain, cotangent):
    vmem, hbm = pl.BlockSpec(memory_space=pltpu.VMEM), pl.BlockSpec(memory_space=pl.ANY)
    scratch = [
        pltpu.VMEM((1, ROWS + 256), jnp.int32),
        pltpu.VMEM((EXT, C), BF),
        pltpu.VMEM((EXT, C), BF),
        pltpu.VMEM((TAPS * C, C), BF),
        pltpu.VMEM((C, C), BF),
        pltpu.VMEM((HALF, HALF), BF),
        pltpu.VMEM((8, C), F32),
        pltpu.VMEM((ROWS, C), F32),
        pltpu.VMEM((ROWS, 128), F32),
        pltpu.VMEM((EXT + 2 * HALO, C), BF),
        pltpu.VMEM((EXT, TAPS * C), BF),
        pltpu.VMEM((2, HALF, ROWS), BF),
        pltpu.VMEM((HALF, ROWS), BF),
        pltpu.VMEM((EXT, WIDE), F32),
        pltpu.VMEM((GROUPS, EXT, WIDE), BF),
        pltpu.VMEM((GROUPS, EXT, WIDE), BF),
        pltpu.VMEM((ROWS, TAPS * C), BF),
        pltpu.VMEM((ROWS, TAPS * WIDE), BF),
        pltpu.VMEM((8, C), F32),
        pltpu.VMEM((TILE, C), F32),
        pltpu.VMEM((TAPS + 1, 8, C), F32),
        pltpu.VMEM((1, C), F32),
        pltpu.VMEM((1, C), F32),
    ]
    scratch += [pltpu.VMEM((GROUPS, TAPS, n, 96, WIDE), BF) for n in (4, 2, 1, 1)]
    scratch += [pltpu.VMEM((GROUPS, 4, TAPS, rows, 128), BF) for rows in (48, 16)]
    scratch += [pltpu.VMEM((GROUPS, 3, TAPS, rows, 128), BF) for rows in (48, 16)]
    scratch += [pltpu.VMEM((4, rows, 128), BF) for rows in BLOCK_ROWS]
    scratch += [pltpu.VMEM((3, rows, 128), BF) for rows in BLOCK_ROWS]
    scratch += [pltpu.VMEM((HALF, 2 * WIDE), F32), pltpu.VMEM((128, WIDE), F32), pltpu.VMEM((96, 128), BF)]
    remotes = 10 + 4 * GROUPS + STAGES
    scratch += [
        pltpu.SemaphoreType.DMA((16,)),
        pltpu.SemaphoreType.DMA((remotes,)),
        pltpu.SemaphoreType.DMA((remotes,)),
    ]
    out, gin, gw, small = pl.pallas_call(
        kernel,
        out_shape=[
            pltpu.VMEM((ROWS, C), BF),
            pltpu.VMEM((ROWS, C), BF),
            pltpu.VMEM((TAPS, 6, C), F32),
            pltpu.VMEM((8, 128), F32),
        ],
        in_specs=[hbm, hbm, vmem, hbm, hbm, hbm, hbm],
        out_specs=[vmem, vmem, vmem, vmem],
        scratch_shapes=scratch,
        compiler_params=pltpu.CompilerParams(collective_id=0, has_side_effects=True, vmem_limit_bytes=58 * 2**20),
        name="block",
    )(
        bases,
        upsampled[0],
        base_table,
        filter_weight.reshape(TAPS * C, C),
        filter_bias,
        norm_gain,
        cotangent[0],
    )
    return out[None], gin[None], gw, small[0, 0:6], small[1, 0:6]


def solution(mesh):
    placed = (P("dp", "seq"), P("dp", "seq", None), P(), P(), P(), P(), P("dp", "seq", None))
    return jax.shard_map(
        body,
        mesh=mesh,
        in_specs=placed,
        out_specs=(
            P("dp", "seq", None),
            P("dp", "seq", None),
            P(None, ("dp", "seq"), None),
            P(("dp", "seq")),
            P(("dp", "seq")),
        ),
        check_vma=False,
    )
```

```python
import jax
import jax.numpy as jnp
import numpy as np
from jax import lax
from jax.experimental import pallas as pl
from jax.experimental.pallas import tpu as pltpu
from jax.sharding import PartitionSpec as P

BF, F32 = jnp.bfloat16, jnp.float32
C, TAPS, STEP = 768, 5, 4
ROWS, HALO = 1024, 16
EXT = ROWS + 2 * HALO
WIDE = 256
GROUPS = C // WIDE
HALF = C // 2
NT = (((1,), (1,)), ((), ()))
TN = (((0,), (0,)), ((), ()))

TAP_OF = [3 * slot % TAPS for slot in range(TAPS)]
SLOTS = ((0, 2), (2, 2), (4, 1))
STAGES = 3
KEPT = ((0, 2, 3, 1), (0, 1, 2, 3))
TILE = 256
BLOCK_ROWS = (96, 32, 16)


def here():
    dp, seq = lax.axis_index("dp"), lax.axis_index("seq")
    return [2 * (dp >> 3) + (seq & 1), (dp >> 1) & 3, seq >> 1], dp & 1, dp, seq


def place(pos, core):
    x, y, z = pos
    return ((x >> 1) * 8 + y * 2 + core, z * 2 + (x & 1))


def moved(pos, axis, to):
    other = list(pos)
    other[axis] = to
    return other


def times(value, step):
    return pl.multiple_of(value * step, step)


def kernel(*refs):
    names = iter(refs)

    def take(n):
        return [next(names) for _ in range(n)]

    bases, up, table, weight, bias_in, gain_in, cot = take(7)
    ob, gi, gw, small = take(4)
    bases_e, up_e, cot_e, w_v, perm_v, permz_v, tab, xs, rin, hb, h5, hs, h_in, pre = take(14)
    gbuf, gpar, g5, g5p, bsum, dh, gws, bias, gain = take(9)
    first_own, first_in, second_own, second_in = take(4)
    blocks, others, bias_blocks, bias_others = [None, *take(2)], [None, *take(2)], take(3), take(3)
    wres, mid, swap_v, w_own = take(4)
    local_sem, send_sem, recv_sem = take(3)

    pos, core, dp, seq = here()
    partner = place(pos, 1 - core)
    left, right = (dp, (seq + 7) & 7), (dp, (seq + 1) & 7)
    onward = {n: [place(moved(pos, a, (pos[a] + n) & 3), core) for a in range(3)] for n in (1, 2, 3)}
    beside = [[place(moved(pos, a, to(pos[a])), core) for a in range(3)] for to in (lambda c: c ^ 1, lambda c: 3 - c)]
    inside = (seq > 0, seq < 7)

    def remote(n, src, dst, device):
        return pltpu.make_async_remote_copy(
            src_ref=src, dst_ref=dst, send_sem=send_sem.at[n], recv_sem=recv_sem.at[n],
            device_id=device, device_id_type=MESH,
        )

    def local(n, src, dst):
        return pltpu.make_async_copy(src, dst, local_sem.at[n])

    in_bases = local(0, bases, bases_e.at[:, pl.ds(128, ROWS)])
    in_up = local(1, up, up_e.at[pl.ds(HALO, ROWS)])
    in_row = [local(2, bias_in, bias.at[0]), local(3, gain_in, gain.at[0])]
    in_w = [local(6 + p, weight.at[:, pl.ds(p * WIDE, WIDE)], w_v.at[:, pl.ds(p * WIDE, WIDE)]) for p in range(GROUPS)]
    in_cot = local(9, cot, cot_e.at[pl.ds(HALO, ROWS)])
    for copy in (in_bases, in_up, *in_row):
        copy.start()

    barrier = pltpu.get_barrier_semaphore()
    partners = [partner, left, right]
    partners += [device for devices in onward.values() for device in devices]
    for device in partners:
        pl.semaphore_signal(barrier, inc=1, device_id=device, device_id_type=MESH)

    halos = [
        remote(0, bases.at[:, pl.ds(ROWS - 128, 128)], bases_e.at[:, pl.ds(0, 128)], right),
        remote(1, bases.at[:, pl.ds(0, 128)], bases_e.at[:, pl.ds(128 + ROWS, 128)], left),
    ]
    for n, (source, target) in enumerate(((up, up_e), (cot, cot_e))):
        halos += [
            remote(2 + 2 * n, source.at[pl.ds(ROWS - HALO, HALO)], target.at[pl.ds(0, HALO)], right),
            remote(3 + 2 * n, source.at[pl.ds(0, HALO)], target.at[pl.ds(HALO + ROWS, HALO)], left),
        ]
    h_copy = remote(6, hs.at[1], h_in, partner)

    def g_copy(p):
        return remote(7 + p, gbuf.at[p], gpar.at[p], partner)

    row = lax.broadcasted_iota(jnp.int32, (HALF, 128), 0)
    column = lax.broadcasted_iota(jnp.int32, (HALF, 128), 1)
    sixth = (row * 10923) >> 16
    last = row - 6 * sixth
    first, second, third = sixth >> 4, (sixth >> 2) & 3, sixth & 3
    channel = (first >> 1) * 384 + second * 96 + third * 12 + (first & 1) * 6 + last
    for n, c in enumerate((core, 1 - core)):
        for b in range(C // 128):
            hit = column + b * 128 == channel + c * 48
            perm_v[n * HALF : (n + 1) * HALF, b * 128 : (b + 1) * 128] = hit.astype(F32).astype(BF)
    turned = second * 96 + third * 24 + first * 6 + last
    for b in range(HALF // 128):
        permz_v[:, b * 128 : (b + 1) * 128] = (column + b * 128 == turned).astype(F32).astype(BF)

    swapped = ((sixth & 3) * 24 + ((sixth >> 2) & 3) * 6 + last)[0:96]
    swap_v[...] = (column[0:96] == swapped).astype(F32).astype(BF)

    tab[...] = jnp.zeros(tab.shape, F32)
    mid[...] = jnp.zeros(mid.shape, F32)
    tab[0:4, :] = table[...].astype(F32)
    bsum[...] = jnp.zeros(bsum.shape, F32)
    code = lax.broadcasted_iota(jnp.int32, (8, 128), 0)

    def embedded(block):
        onehot = (code == bases_e[:, pl.ds(times(block, 128), 128)]).astype(F32)
        return lax.dot_general(onehot, tab[...], TN, preferred_element_type=F32)

    def normed_of(x):
        r = lax.rsqrt(jnp.mean(x * x, axis=-1, keepdims=True) + 1e-06)
        return r, (x * r * gain[...])

    def norm_block(pair, carry):
        both = [embedded(2 * pair + 1), embedded(2 * pair + 2)]
        for s in range(8):
            row = pl.multiple_of(pair * 256 + s * 32, 32)
            x = up_e[pl.ds(row + HALO, 32), :].astype(F32) + both[s // 4][s % 4 * 32 : s % 4 * 32 + 32]
            r, h = normed_of(x)
            xs[pl.ds(row, 32), :] = x
            rin[pl.ds(row, 32), :] = jnp.broadcast_to(r, (32, 128))
            hb[pl.ds(row + 2 * HALO, 32), :] = h.astype(BF)
        return carry

    def norm():
        for copy in (in_bases, in_up, *in_row):
            copy.wait()
        for copy in (*in_w, in_cot):
            copy.start()
        lax.fori_loop(0, ROWS // 256, norm_block, 0)
        pl.semaphore_wait(barrier, len(partners))
        for copy in halos:
            copy.start()

    def norm_ends():
        for copy in halos:
            copy.wait_recv()
        hb[0:HALO, :] = jnp.zeros((HALO, C), BF)
        hb[HALO + EXT : 2 * HALO + EXT, :] = jnp.zeros((HALO, C), BF)
        for side, (block, skip) in enumerate(((0, 128 - HALO), (1 + ROWS // 128, 0))):
            start = side * (HALO + ROWS)
            x = up_e[start : start + HALO, :].astype(F32) + embedded(block)[skip : skip + HALO]
            h = jnp.where(inside[side], normed_of(x)[1], 0.0)
            hb[start + HALO : start + 2 * HALO, :] = h.astype(BF)

    def turn():
        for n in range(2):
            rows = perm_v[(1 - n) * HALF : (2 - n) * HALF, :]
            h_own = hb[2 * HALO : 2 * HALO + ROWS, :]
            hs[1 - n] = lax.dot_general(rows, h_own, NT, preferred_element_type=F32).astype(BF)
            if n == 0:
                h_copy.start()


    def shift_h():
        def tile(j, carry):
            row = times(j, 96)
            for p in range(GROUPS):
                v = hb[pl.ds(row, 128), p * WIDE : (p + 1) * WIDE].astype(F32)
                for k in range(TAPS):
                    h5[pl.ds(row, 96), k * C + p * WIDE : k * C + (p + 1) * WIDE] = v[8 + STEP * k : 104 + STEP * k].astype(BF)
            return carry

        lax.fori_loop(0, EXT // 96, tile, 0)

    c0 = np.float32(np.sqrt(2 / np.pi))

    def gelu_pair(z):
        square = z * z
        t = jnp.tanh(c0 * z * (1 + 0.044715 * square))
        cdf = 0.5 + 0.5 * t
        slope = cdf + (0.5 * c0) * z * (1 - t * t) * (1 + 0.134145 * square)
        return z * cdf, slope

    def forward(p):
        cols = pl.ds(times(p, WIDE), WIDE)
        for n in range(GROUPS):
            pl.when(p == n)(in_w[n].wait)
        pl.when(p == 0)(in_cot.wait)
        half = EXT // 2

        def tile(row, n):
            act, slope = gelu_pair(pre[row + HALO : row + HALO + n, :] + bias[:, cols])
            ob[row : row + n, cols] = (xs[row : row + n, cols] + act).astype(BF)
            gbuf[p, row + HALO : row + HALO + n, :] = (cot_e[row + HALO : row + HALO + n, cols].astype(F32) * slope).astype(BF)

        pre[0:half, :] = jnp.dot(h5[0:half, :], w_v[:, cols], preferred_element_type=F32)
        for row in range(0, half - HALO, 64):
            tile(row, 64)
        pre[half:, :] = jnp.dot(h5[half:, :], w_v[:, cols], preferred_element_type=F32)
        for row in range(half - HALO, ROWS, 64):
            tile(row, 64)
        for side in range(2):
            rows = slice(side * (HALO + ROWS), side * (HALO + ROWS) + HALO)
            _, slope = gelu_pair(pre[rows, :] + bias[:, cols])
            g = jnp.where(inside[side], cot_e[rows, cols].astype(F32) * slope, 0.0)
            gbuf[p, rows, :] = g.astype(BF)
        g_copy(p).start()

    def shift_g(source, p, target, column):
        def tile(j, total):
            row = times(j, 128)
            v = source[p, pl.ds(row, 160), :].astype(F32)
            for k in range(TAPS):
                target[pl.ds(row, 128), pl.ds(column(k), WIDE)] = v[24 - STEP * k : 152 - STEP * k].astype(BF)
            return total + jnp.sum(v[16:144].reshape(16, 8, WIDE), axis=0)

        bsum[:, pl.ds(times(p, WIDE), WIDE)] += lax.fori_loop(0, ROWS // 128, tile, jnp.zeros((8, WIDE), F32))

    def axis_of(kind, stage):
        return jnp.where(kind + stage >= 3, kind + stage - 3, kind + stage)

    def pick_of(axis, three):
        return jnp.where(axis == 0, three[0], jnp.where(axis == 1, three[1], three[2]))

    def along(axis):
        return pick_of(axis, pos)

    def device_of(axis, three):
        return tuple(pick_of(axis, [device[n] for device in three]) for n in range(2))

    def kind_of(p, m):
        return jnp.where(p + m >= 3, p + m - 3, p + m)

    def step_sem(p, step):
        return 10 + 4 * p + step

    def step_wait(p, step):
        whole = (first_in, second_in, others[1], others[2])[step].at[p]
        return remote(step_sem(p, step), whole, whole, partner)

    def hops(n, axis, source, target):
        c = along(axis)
        return [
            remote(n, source((c + delta) & 3), target(delta - 1), device_of(axis, onward[delta])) for delta in (1, 2, 3)
        ]

    def kept_set(c, odd):
        return c >> 1 if odd else ((c + 1) >> 1) & 1

    def mine_of(c, odd):
        return c & 1 if odd else c >> 1

    def pair_copy(p, m, n, step):
        kind, slot, odd = kind_of(p, m), 2 * m + n, n
        c = along(kind)
        flip = (step == 0) == (odd == 0)
        other = device_of(kind, beside[0 if flip else 1])
        if step == 0:
            to = c ^ 1 if flip else 3 - c
            source = first_own.at[p, slot, pl.ds(2 * kept_set(to, odd), 2)]
            return remote(step_sem(p, step), source, first_in.at[p, slot], other)
        return remote(step_sem(p, step), second_own.at[p, slot], second_in.at[p, slot], other)

    def piece_hops(p, m, stage):
        slot, count = SLOTS[m]
        return hops(
            step_sem(p, stage + 1),
            axis_of(kind_of(p, m), stage),
            lambda d: blocks[stage].at[p, d, pl.ds(slot, count)],
            lambda d: others[stage].at[p, d, pl.ds(slot, count)],
        )

    def bias_hops(stage):
        return hops(
            22 + stage,
            jnp.int32(stage),
            lambda d: bias_blocks[stage].at[d],
            lambda d: bias_others[stage].at[d],
        )

    def bias_wait(stage):
        return remote(22 + stage, bias_others[stage], bias_others[stage], partner)

    def weights(p):
        shift_g(gbuf, p, g5, lambda k: pl.multiple_of(k * C + p * WIDE, WIDE))
        g_copy(p).wait_recv()
        shift_g(gpar, p, g5p, lambda k: TAP_OF.index(k) * WIDE)

        @pl.when(p == 0)
        def _():
            h_copy.wait_recv()

        def piece(m, first, count):
            own = [g5[:, pl.ds(pl.multiple_of(lax.rem(3 * (first + n), TAPS) * C + p * WIDE, WIDE), WIDE)] for n in range(count)]
            other = g5p[:, pl.ds(times(first, WIDE), count * WIDE)]
            rhs = jnp.concatenate([jnp.concatenate(own, axis=1) if count > 1 else own[0], other], axis=0)
            lhs = jnp.concatenate([hs[0], h_in[...]], axis=1)
            wres[:, 0 : count * WIDE] = jnp.dot(lhs, rhs, preferred_element_type=F32)
            kind = kind_of(p, m)
            wide = count * WIDE

            def store(block):
                for d in range(4):
                    rows = block(d).astype(BF)
                    for n in range(count):
                        first_own[p, first + n, KEPT[n][d]] = rows[:, n * WIDE : (n + 1) * WIDE]

            @pl.when(kind == 0)
            def _():
                store(lambda d: wres[d * 96 : d * 96 + 96, 0:wide])

            @pl.when(kind == 1)
            def _():
                store(lambda d: jnp.concatenate([wres[e * 96 + d * 24 : e * 96 + d * 24 + 24, 0:wide] for e in range(4)], axis=0))

            @pl.when(kind == 2)
            def _():
                r = jnp.dot(permz_v[...], wres[:, 0:wide].astype(BF), preferred_element_type=F32)
                store(lambda d: r[d * 96 : d * 96 + 96])

            for n in range(count):
                pair_copy(p, m, n, 0).start()

        def pair(m, carry):
            piece(m, 2 * m, 2)
            return carry

        lax.fori_loop(0, 2, pair, 0)
        piece(2, 4, 1)

        @pl.when(p == GROUPS - 1)
        def _():
            total = jnp.sum(bsum[...], axis=0, keepdims=True)
            total = jnp.broadcast_to(total, (128, C)).astype(BF)
            r = lax.dot_general(perm_v[0:HALF, :], total, NT, preferred_element_type=F32)
            for d in range(4):
                bias_blocks[0][d] = r[d * 96 : d * 96 + 96].astype(BF)
            for copy in bias_hops(0):
                copy.start()

    def spread_of(shape, sixteenth):
        r, c = lax.broadcasted_iota(jnp.int32, shape, 0), lax.broadcasted_iota(jnp.int32, shape, 1)
        return sixteenth(c, 6 * (r >> 4), r & 15).astype(F32).astype(BF)

    spread = spread_of((64, 32), lambda c, base, w: (w < 6) & (c == base + w))
    spread_two = spread_of((64, 48), lambda c, base, w: ((w & 7) < 6) & (c == base + (w & 7) + 24 * (w >> 3)))

    def handed_on(total, stage, store):
        if stage == 0:
            for d in range(4):
                block = jnp.concatenate([total[24 * d : 24 * d + 24], jnp.zeros((8, total.shape[1]), F32)], axis=0)
                store(d, block.astype(BF))
        else:
            r = jnp.dot(spread, total.astype(BF), preferred_element_type=F32).astype(BF)
            for d in range(4):
                store(d, r[16 * d : 16 * d + 16])

    def finish_first(p, step):
        step_wait(p, step).wait_recv()
        for m, (first, count) in enumerate(SLOTS):
            c = along(kind_of(p, m))
            for slot in range(first, first + count):
                odd = slot % 2
                mine = mine_of(c, odd)
                if step == 0:
                    mine = 1 - mine
                total = first_own[p, slot, 2 * kept_set(c, odd) + mine].astype(F32) + first_in[p, slot, mine].astype(F32)
                if step == 0:
                    second_own[p, slot, 0] = total.astype(BF)
                    pair_copy(p, m, odd, 1).start()
                else:
                    mid[0:96, :] = total + second_in[p, slot, 0].astype(F32)

                    @pl.when(kind_of(p, m) == 1)
                    def _():
                        mid[0:96, :] = jnp.dot(swap_v[...], mid[...].astype(BF), preferred_element_type=F32)

                    for d in range(4):
                        rows = mid[24 * d : 24 * d + 24, :]
                        block = jnp.concatenate([rows[:, 0:128], rows[:, 128:]], axis=0)
                        blocks[1][p, d, slot] = block.astype(BF)
            if step == 1:
                for copy in piece_hops(p, m, 1):
                    copy.start()

    def finish_next(p, stage):
        step_wait(p, stage + 1).wait_recv()
        for m, (first, count) in enumerate(SLOTS):
            own = along(axis_of(kind_of(p, m), stage))
            for slot in range(first, first + count):
                total = blocks[stage][p, own, slot].astype(F32)
                for d in range(3):
                    total = total + others[stage][p, d, slot].astype(F32)
                if stage == 1:
                    r = jnp.dot(spread_two, total.astype(BF), preferred_element_type=F32).astype(BF)
                    for d in range(4):
                        blocks[2][p, d, slot] = r[16 * d : 16 * d + 16]
                else:
                    for half in range(2):
                        gws[TAP_OF[slot], :, pl.ds(times(2 * p + half, 128), 128)] = total[8 * half : 8 * half + 8]
            if stage == 1:
                for copy in piece_hops(p, m, 2):
                    copy.start()

    def finish(p, step):
        if step < 2:
            finish_first(p, step)
        else:
            finish_next(p, step - 1)

    def finish_bias(stage):
        bias_wait(stage).wait_recv()
        total = bias_blocks[stage][pos[stage]].astype(F32)
        for d in range(3):
            total = total + bias_others[stage][d].astype(F32)
        if stage == 2:
            gws[TAPS, :, 0:128] = total[0:8]
        else:

            def store(d, value):
                bias_blocks[stage + 1][d] = value

            handed_on(total, stage, store)
            for copy in bias_hops(stage + 1):
                copy.start()

    def hidden(t):
        rows = pl.ds(times(t, TILE), TILE)
        return sum(
            lax.dot_general(g5[rows, k * C : (k + 1) * C], w_v[k * C : (k + 1) * C, :], NT, preferred_element_type=F32)
            for k in range(TAPS)
        )

    def input_gradient(t):
        for i in range(TILE // 32):
            row = pl.multiple_of(t * TILE + i * 32, 32)
            r = jnp.concatenate([rin[pl.ds(row, 32), :]] * (C // 128), axis=1)
            normed = xs[pl.ds(row, 32), :] * r
            dn = dh[i * 32 : i * 32 + 32, :] * gain[...]
            mean = jnp.mean(dn * normed, axis=-1, keepdims=True)
            g = cot_e[pl.ds(row + HALO, 32), :].astype(F32) + (dn - normed * mean) * r
            gi[pl.ds(row, 32), :] = g.astype(BF)

    def backward(t):
        input_gradient(jnp.maximum(t - 1, 0))
        dh[...] = hidden(t)

    mine = (dp * 8 + seq) * 6

    def own_weights():
        base = jnp.minimum((mine >> 4) * 16, C - 32)
        pick_row = lax.broadcasted_iota(jnp.int32, (8, 32), 0)
        pick_col = lax.broadcasted_iota(jnp.int32, (8, 32), 1)
        pick = (pick_col == pick_row + (mine - base)).astype(F32).astype(BF)
        for k in range(TAPS):
            rows = w_v[pl.ds(pl.multiple_of(k * C + base, 16), 32), :]
            w_own[k] = jnp.dot(pick, rows, preferred_element_type=F32)

    def before_last():
        input_gradient(ROWS // TILE - 1)
        for copy in (*halos, h_copy):
            copy.wait_send()
        for p in range(GROUPS):
            g_copy(p).wait_send()
        for p in range(GROUPS - 1):
            for step in range(4):
                step_wait(p, step).wait_send()

    def during(s, start, stop, step):
        if stop > start:
            pl.when((s >= start) & (s < stop))(step)

    def turn_of(s, carry):
        during(s, 0, 3, lambda: forward(s))
        during(s, 1, 4, lambda: weights(s - 1))
        during(s, 4, 8, lambda: backward(s - 4))
        during(s, 6, 7, own_weights)
        during(s, 7, 8, before_last)
        for step in range(4):
            during(s, 2 + step, 5 + step, lambda: finish(s - 2 - step, step))
            if step < 3:
                during(s, 5 + step, 6 + step, lambda: finish_bias(step))
        return carry

    norm()
    turn()
    norm_ends()
    shift_h()
    dh[...] = jnp.zeros(dh.shape, F32)
    lax.fori_loop(0, 8, turn_of, 0)

    gw[...] = gws[0:TAPS, 0:6, :]
    total = jnp.zeros((8, C), F32)
    for k in range(TAPS):
        total = total + w_own[k] * gws[k]
    lane = lax.broadcasted_iota(jnp.int32, (8, C), 1)
    row = lax.broadcasted_iota(jnp.int32, (8, C), 0)
    own_gain = jnp.sum(jnp.where(lane == row + mine, gain[...], 0.0), axis=-1, keepdims=True)
    column = jnp.sum(total, axis=-1, keepdims=True) / own_gain
    diagonal = (lane == row)[:, 0:128] & (row < 6)[:, 0:128]
    small[0:1, :] = jnp.sum(jnp.where(diagonal, gws[TAPS, :, 0:128], 0.0), axis=0, keepdims=True)
    small[1:2, :] = jnp.sum(jnp.where(diagonal, column, 0.0), axis=0, keepdims=True)

    for stage in range(STAGES):
        bias_wait(stage).wait_send()
    for step in range(4):
        step_wait(GROUPS - 1, step).wait_send()


MESH = pl.DeviceIdType.MESH


def body(bases, upsampled, base_table, filter_weight, filter_bias, norm_gain, cotangent):
    vmem, hbm = pl.BlockSpec(memory_space=pltpu.VMEM), pl.BlockSpec(memory_space=pl.ANY)
    scratch = [
        pltpu.VMEM((1, ROWS + 256), jnp.int32),
        pltpu.VMEM((EXT, C), BF),
        pltpu.VMEM((EXT, C), BF),
        pltpu.VMEM((TAPS * C, C), BF),
        pltpu.VMEM((C, C), BF),
        pltpu.VMEM((HALF, HALF), BF),
        pltpu.VMEM((8, C), F32),
        pltpu.VMEM((ROWS, C), F32),
        pltpu.VMEM((ROWS, 128), F32),
        pltpu.VMEM((EXT + 2 * HALO, C), BF),
        pltpu.VMEM((EXT, TAPS * C), BF),
        pltpu.VMEM((2, HALF, ROWS), BF),
        pltpu.VMEM((HALF, ROWS), BF),
        pltpu.VMEM((EXT, WIDE), F32),
        pltpu.VMEM((GROUPS, EXT, WIDE), BF),
        pltpu.VMEM((GROUPS, EXT, WIDE), BF),
        pltpu.VMEM((ROWS, TAPS * C), BF),
        pltpu.VMEM((ROWS, TAPS * WIDE), BF),
        pltpu.VMEM((8, C), F32),
        pltpu.VMEM((TILE, C), F32),
        pltpu.VMEM((TAPS + 1, 8, C), F32),
        pltpu.VMEM((1, C), F32),
        pltpu.VMEM((1, C), F32),
    ]
    scratch += [pltpu.VMEM((GROUPS, TAPS, n, 96, WIDE), BF) for n in (4, 2, 1, 1)]
    scratch += [pltpu.VMEM((GROUPS, 4, TAPS, rows, 128), BF) for rows in (48, 16)]
    scratch += [pltpu.VMEM((GROUPS, 3, TAPS, rows, 128), BF) for rows in (48, 16)]
    scratch += [pltpu.VMEM((4, rows, 128), BF) for rows in BLOCK_ROWS]
    scratch += [pltpu.VMEM((3, rows, 128), BF) for rows in BLOCK_ROWS]
    scratch += [pltpu.VMEM((HALF, 2 * WIDE), F32), pltpu.VMEM((128, WIDE), F32), pltpu.VMEM((96, 128), BF)]
    scratch += [pltpu.VMEM((TAPS, 8, C), F32)]
    remotes = 10 + 4 * GROUPS + STAGES
    scratch += [
        pltpu.SemaphoreType.DMA((16,)),
        pltpu.SemaphoreType.DMA((remotes,)),
        pltpu.SemaphoreType.DMA((remotes,)),
    ]
    out, gin, gw, small = pl.pallas_call(
        kernel,
        out_shape=[
            pltpu.VMEM((ROWS, C), BF),
            pltpu.VMEM((ROWS, C), BF),
            pltpu.VMEM((TAPS, 6, C), F32),
            pltpu.VMEM((8, 128), F32),
        ],
        in_specs=[hbm, hbm, vmem, hbm, hbm, hbm, hbm],
        out_specs=[vmem, vmem, vmem, vmem],
        scratch_shapes=scratch,
        compiler_params=pltpu.CompilerParams(collective_id=0, has_side_effects=True, vmem_limit_bytes=58 * 2**20),
        name="block",
    )(
        bases,
        upsampled[0],
        base_table,
        filter_weight.reshape(TAPS * C, C),
        filter_bias,
        norm_gain,
        cotangent[0],
    )
    return out[None], gin[None], gw, small[0, 0:6], small[1, 0:6]


def solution(mesh):
    placed = (P("dp", "seq"), P("dp", "seq", None), P(), P(), P(), P(), P("dp", "seq", None))
    return jax.shard_map(
        body,
        mesh=mesh,
        in_specs=placed,
        out_specs=(
            P("dp", "seq", None),
            P("dp", "seq", None),
            P(None, ("dp", "seq"), None),
            P(("dp", "seq")),
            P(("dp", "seq")),
        ),
        check_vma=False,
    )
```

```python
import jax
import jax.numpy as jnp
import numpy as np
from jax import lax
from jax.experimental import pallas as pl
from jax.experimental.pallas import tpu as pltpu
from jax.sharding import PartitionSpec as P

BF, F32 = jnp.bfloat16, jnp.float32
C, TAPS, STEP = 768, 5, 4
ROWS, HALO = 1024, 16
EXT = ROWS + 2 * HALO
WIDE = 256
GROUPS = C // WIDE
HALF = C // 2
NT = (((1,), (1,)), ((), ()))
TN = (((0,), (0,)), ((), ()))

TAP_OF = [3 * slot % TAPS for slot in range(TAPS)]
SLOTS = ((0, 2), (2, 2), (4, 1))
STAGES = 3
KEPT = ((0, 2, 3, 1), (0, 1, 2, 3))
TILE = 256
BLOCK_ROWS = (96, 32, 16)


def here():
    dp, seq = lax.axis_index("dp"), lax.axis_index("seq")
    return [2 * (dp >> 3) + (seq & 1), (dp >> 1) & 3, seq >> 1], dp & 1, dp, seq


def place(pos, core):
    x, y, z = pos
    return ((x >> 1) * 8 + y * 2 + core, z * 2 + (x & 1))


def moved(pos, axis, to):
    other = list(pos)
    other[axis] = to
    return other


def times(value, step):
    return pl.multiple_of(value * step, step)


def kernel(*refs):
    names = iter(refs)

    def take(n):
        return [next(names) for _ in range(n)]

    bases, up, table, weight, bias_in, gain_in, cot = take(7)
    ob, gi, gw, small = take(4)
    bases_e, up_e, cot_e, w_v, perm_v, permz_v, tab, xs, rin, hb, h5, hs, h_in, pre = take(14)
    gbuf, gpar, g5, g5p, bsum, dh, gws, bias, gain = take(9)
    first_own, first_in, second_own, second_in = take(4)
    blocks, others, bias_blocks, bias_others = [None, *take(2)], [None, *take(2)], take(3), take(3)
    wres, mid, swap_v, w_own = take(4)
    local_sem, send_sem, recv_sem = take(3)

    pos, core, dp, seq = here()
    partner = place(pos, 1 - core)
    left, right = (dp, (seq + 7) & 7), (dp, (seq + 1) & 7)
    onward = {n: [place(moved(pos, a, (pos[a] + n) & 3), core) for a in range(3)] for n in (1, 2, 3)}
    beside = [[place(moved(pos, a, to(pos[a])), core) for a in range(3)] for to in (lambda c: c ^ 1, lambda c: 3 - c)]
    inside = (seq > 0, seq < 7)

    def remote(n, src, dst, device):
        return pltpu.make_async_remote_copy(
            src_ref=src, dst_ref=dst, send_sem=send_sem.at[n], recv_sem=recv_sem.at[n],
            device_id=device, device_id_type=MESH,
        )

    def local(n, src, dst):
        return pltpu.make_async_copy(src, dst, local_sem.at[n])

    in_bases = local(0, bases, bases_e.at[:, pl.ds(128, ROWS)])
    in_up = local(1, up, up_e.at[pl.ds(HALO, ROWS)])
    in_row = [local(2, bias_in, bias.at[0]), local(3, gain_in, gain.at[0])]
    in_w = [local(6 + p, weight.at[:, pl.ds(p * WIDE, WIDE)], w_v.at[:, pl.ds(p * WIDE, WIDE)]) for p in range(GROUPS)]
    in_cot = local(9, cot, cot_e.at[pl.ds(HALO, ROWS)])
    for copy in (in_bases, in_up, *in_row):
        copy.start()

    barrier = pltpu.get_barrier_semaphore()
    partners = [partner, left, right]
    partners += [device for devices in onward.values() for device in devices]
    for device in partners:
        pl.semaphore_signal(barrier, inc=1, device_id=device, device_id_type=MESH)

    halos = [
        remote(0, bases.at[:, pl.ds(ROWS - 128, 128)], bases_e.at[:, pl.ds(0, 128)], right),
        remote(1, bases.at[:, pl.ds(0, 128)], bases_e.at[:, pl.ds(128 + ROWS, 128)], left),
    ]
    for n, (source, target) in enumerate(((up, up_e), (cot, cot_e))):
        halos += [
            remote(2 + 2 * n, source.at[pl.ds(ROWS - HALO, HALO)], target.at[pl.ds(0, HALO)], right),
            remote(3 + 2 * n, source.at[pl.ds(0, HALO)], target.at[pl.ds(HALO + ROWS, HALO)], left),
        ]
    h_copy = remote(6, hs.at[1], h_in, partner)

    def g_copy(p):
        return remote(7 + p, gbuf.at[p], gpar.at[p], partner)

    row = lax.broadcasted_iota(jnp.int32, (HALF, 128), 0)
    column = lax.broadcasted_iota(jnp.int32, (HALF, 128), 1)
    sixth = (row * 10923) >> 16
    last = row - 6 * sixth
    first, second, third = sixth >> 4, (sixth >> 2) & 3, sixth & 3
    channel = (first >> 1) * 384 + second * 96 + third * 12 + (first & 1) * 6 + last
    for n, c in enumerate((core, 1 - core)):
        for b in range(C // 128):
            hit = column + b * 128 == channel + c * 48
            perm_v[n * HALF : (n + 1) * HALF, b * 128 : (b + 1) * 128] = hit.astype(F32).astype(BF)
    turned = second * 96 + third * 24 + first * 6 + last
    for b in range(HALF // 128):
        permz_v[:, b * 128 : (b + 1) * 128] = (column + b * 128 == turned).astype(F32).astype(BF)

    swapped = ((sixth & 3) * 24 + ((sixth >> 2) & 3) * 6 + last)[0:96]
    swap_v[...] = (column[0:96] == swapped).astype(F32).astype(BF)

    tab[...] = jnp.zeros(tab.shape, F32)
    mid[...] = jnp.zeros(mid.shape, F32)
    tab[0:4, :] = table[...].astype(F32)
    bsum[...] = jnp.zeros(bsum.shape, F32)
    code = lax.broadcasted_iota(jnp.int32, (8, 128), 0)

    def embedded(block):
        onehot = (code == bases_e[:, pl.ds(times(block, 128), 128)]).astype(F32)
        return lax.dot_general(onehot, tab[...], TN, preferred_element_type=F32)

    def normed_of(x):
        r = lax.rsqrt(jnp.mean(x * x, axis=-1, keepdims=True) + 1e-06)
        return r, (x * r * gain[...])

    def norm_block(pair, carry):
        both = [embedded(2 * pair + 1), embedded(2 * pair + 2)]
        for s in range(8):
            row = pl.multiple_of(pair * 256 + s * 32, 32)
            x = up_e[pl.ds(row + HALO, 32), :].astype(F32) + both[s // 4][s % 4 * 32 : s % 4 * 32 + 32]
            r, h = normed_of(x)
            xs[pl.ds(row, 32), :] = x
            rin[pl.ds(row, 32), :] = jnp.broadcast_to(r, (32, 128))
            hb[pl.ds(row + 2 * HALO, 32), :] = h.astype(BF)
        return carry

    def norm():
        for copy in (in_bases, in_up, *in_row):
            copy.wait()
        for copy in (*in_w, in_cot):
            copy.start()
        lax.fori_loop(0, ROWS // 256, norm_block, 0)
        pl.semaphore_wait(barrier, len(partners))
        for copy in halos:
            copy.start()

    def norm_ends():
        for copy in halos:
            copy.wait_recv()
        hb[0:HALO, :] = jnp.zeros((HALO, C), BF)
        hb[HALO + EXT : 2 * HALO + EXT, :] = jnp.zeros((HALO, C), BF)
        for side, (block, skip) in enumerate(((0, 128 - HALO), (1 + ROWS // 128, 0))):
            start = side * (HALO + ROWS)
            x = up_e[start : start + HALO, :].astype(F32) + embedded(block)[skip : skip + HALO]
            h = jnp.where(inside[side], normed_of(x)[1], 0.0)
            hb[start + HALO : start + 2 * HALO, :] = h.astype(BF)

    def turn():
        for n in range(2):
            rows = perm_v[(1 - n) * HALF : (2 - n) * HALF, :]
            h_own = hb[2 * HALO : 2 * HALO + ROWS, :]
            hs[1 - n] = lax.dot_general(rows, h_own, NT, preferred_element_type=F32).astype(BF)
            if n == 0:
                h_copy.start()


    def shift_h():
        def tile(j, carry):
            row = times(j, 96)
            for p in range(GROUPS):
                v = hb[pl.ds(row, 128), p * WIDE : (p + 1) * WIDE].astype(F32)
                for k in range(TAPS):
                    h5[pl.ds(row, 96), k * C + p * WIDE : k * C + (p + 1) * WIDE] = v[8 + STEP * k : 104 + STEP * k].astype(BF)
            return carry

        lax.fori_loop(0, EXT // 96, tile, 0)

    c0 = np.float32(np.sqrt(2 / np.pi))

    def gelu_pair(z):
        square = z * z
        t = jnp.tanh(c0 * z * (1 + 0.044715 * square))
        cdf = 0.5 + 0.5 * t
        slope = cdf + (0.5 * c0) * z * (1 - t * t) * (1 + 0.134145 * square)
        return z * cdf, slope

    def forward(p):
        cols = pl.ds(times(p, WIDE), WIDE)
        for n in range(GROUPS):
            pl.when(p == n)(in_w[n].wait)
        pl.when(p == 0)(in_cot.wait)
        half = EXT // 2

        def tile(row, n):
            act, slope = gelu_pair(pre[row + HALO : row + HALO + n, :] + bias[:, cols])
            ob[row : row + n, cols] = (xs[row : row + n, cols] + act).astype(BF)
            gbuf[p, row + HALO : row + HALO + n, :] = (cot_e[row + HALO : row + HALO + n, cols].astype(F32) * slope).astype(BF)

        pre[0:half, :] = jnp.dot(h5[0:half, :], w_v[:, cols], preferred_element_type=F32)
        for row in range(0, half - HALO, 64):
            tile(row, 64)
        pre[half:, :] = jnp.dot(h5[half:, :], w_v[:, cols], preferred_element_type=F32)
        for row in range(half - HALO, ROWS, 64):
            tile(row, 64)
        for side in range(2):
            rows = slice(side * (HALO + ROWS), side * (HALO + ROWS) + HALO)
            _, slope = gelu_pair(pre[rows, :] + bias[:, cols])
            g = jnp.where(inside[side], cot_e[rows, cols].astype(F32) * slope, 0.0)
            gbuf[p, rows, :] = g.astype(BF)
        g_copy(p).start()

    def shift_g(source, p, target, column):
        def tile(j, total):
            row = times(j, 128)
            v = source[p, pl.ds(row, 160), :].astype(F32)
            for k in range(TAPS):
                target[pl.ds(row, 128), pl.ds(column(k), WIDE)] = v[24 - STEP * k : 152 - STEP * k].astype(BF)
            return total + jnp.sum(v[16:144].reshape(16, 8, WIDE), axis=0)

        bsum[:, pl.ds(times(p, WIDE), WIDE)] += lax.fori_loop(0, ROWS // 128, tile, jnp.zeros((8, WIDE), F32))

    def axis_of(kind, stage):
        return jnp.where(kind + stage >= 3, kind + stage - 3, kind + stage)

    def pick_of(axis, three):
        return jnp.where(axis == 0, three[0], jnp.where(axis == 1, three[1], three[2]))

    def along(axis):
        return pick_of(axis, pos)

    def device_of(axis, three):
        return tuple(pick_of(axis, [device[n] for device in three]) for n in range(2))

    def kind_of(p, m):
        return jnp.where(p + m >= 3, p + m - 3, p + m)

    def step_sem(p, step):
        return 10 + 4 * p + step

    def step_wait(p, step):
        whole = (first_in, second_in, others[1], others[2])[step].at[p]
        return remote(step_sem(p, step), whole, whole, partner)

    def hops(n, axis, source, target):
        c = along(axis)
        return [
            remote(n, source((c + delta) & 3), target(delta - 1), device_of(axis, onward[delta])) for delta in (1, 2, 3)
        ]

    def kept_set(c, odd):
        return c >> 1 if odd else ((c + 1) >> 1) & 1

    def mine_of(c, odd):
        return c & 1 if odd else c >> 1

    def pair_copy(p, m, n, step):
        kind, slot, odd = kind_of(p, m), 2 * m + n, n
        c = along(kind)
        flip = (step == 0) == (odd == 0)
        other = device_of(kind, beside[0 if flip else 1])
        if step == 0:
            to = c ^ 1 if flip else 3 - c
            source = first_own.at[p, slot, pl.ds(2 * kept_set(to, odd), 2)]
            return remote(step_sem(p, step), source, first_in.at[p, slot], other)
        return remote(step_sem(p, step), second_own.at[p, slot], second_in.at[p, slot], other)

    def piece_hops(p, m, stage):
        slot, count = SLOTS[m]
        return hops(
            step_sem(p, stage + 1),
            axis_of(kind_of(p, m), stage),
            lambda d: blocks[stage].at[p, d, pl.ds(slot, count)],
            lambda d: others[stage].at[p, d, pl.ds(slot, count)],
        )

    def bias_hops(stage):
        return hops(
            22 + stage,
            jnp.int32(stage),
            lambda d: bias_blocks[stage].at[d],
            lambda d: bias_others[stage].at[d],
        )

    def bias_wait(stage):
        return remote(22 + stage, bias_others[stage], bias_others[stage], partner)

    def weights(p):
        shift_g(gbuf, p, g5, lambda k: pl.multiple_of(k * C + p * WIDE, WIDE))
        g_copy(p).wait_recv()
        shift_g(gpar, p, g5p, lambda k: TAP_OF.index(k) * WIDE)

        @pl.when(p == 0)
        def _():
            h_copy.wait_recv()

        def piece(m, first, count):
            own = [g5[:, pl.ds(pl.multiple_of(lax.rem(3 * (first + n), TAPS) * C + p * WIDE, WIDE), WIDE)] for n in range(count)]
            other = g5p[:, pl.ds(times(first, WIDE), count * WIDE)]
            rhs = jnp.concatenate([jnp.concatenate(own, axis=1) if count > 1 else own[0], other], axis=0)
            lhs = jnp.concatenate([hs[0], h_in[...]], axis=1)
            wres[:, 0 : count * WIDE] = jnp.dot(lhs, rhs, preferred_element_type=F32)
            kind = kind_of(p, m)
            wide = count * WIDE

            def store(block):
                for d in range(4):
                    rows = block(d).astype(BF)
                    for n in range(count):
                        first_own[p, first + n, KEPT[n][d]] = rows[:, n * WIDE : (n + 1) * WIDE]

            @pl.when(kind == 0)
            def _():
                store(lambda d: wres[d * 96 : d * 96 + 96, 0:wide])

            @pl.when(kind == 1)
            def _():
                store(lambda d: jnp.concatenate([wres[e * 96 + d * 24 : e * 96 + d * 24 + 24, 0:wide] for e in range(4)], axis=0))

            @pl.when(kind == 2)
            def _():
                r = jnp.dot(permz_v[...], wres[:, 0:wide].astype(BF), preferred_element_type=F32)
                store(lambda d: r[d * 96 : d * 96 + 96])

            for n in range(count):
                pair_copy(p, m, n, 0).start()

        def pair(m, carry):
            piece(m, 2 * m, 2)
            return carry

        lax.fori_loop(0, 2, pair, 0)
        piece(2, 4, 1)

        @pl.when(p == GROUPS - 1)
        def _():
            total = jnp.sum(bsum[...], axis=0, keepdims=True)
            total = jnp.broadcast_to(total, (128, C)).astype(BF)
            r = lax.dot_general(perm_v[0:HALF, :], total, NT, preferred_element_type=F32)
            for d in range(4):
                bias_blocks[0][d] = r[d * 96 : d * 96 + 96].astype(BF)
            for copy in bias_hops(0):
                copy.start()

    def spread_of(shape, sixteenth):
        r, c = lax.broadcasted_iota(jnp.int32, shape, 0), lax.broadcasted_iota(jnp.int32, shape, 1)
        return sixteenth(c, 6 * (r >> 4), r & 15).astype(F32).astype(BF)

    spread = spread_of((64, 32), lambda c, base, w: (w < 6) & (c == base + w))
    spread_two = spread_of((64, 48), lambda c, base, w: ((w & 7) < 6) & (c == base + (w & 7) + 24 * (w >> 3)))

    def handed_on(total, stage, store):
        if stage == 0:
            for d in range(4):
                block = jnp.concatenate([total[24 * d : 24 * d + 24], jnp.zeros((8, total.shape[1]), F32)], axis=0)
                store(d, block.astype(BF))
        else:
            r = jnp.dot(spread, total.astype(BF), preferred_element_type=F32).astype(BF)
            for d in range(4):
                store(d, r[16 * d : 16 * d + 16])

    def finish_first(p, step):
        step_wait(p, step).wait_recv()
        for m, (first, count) in enumerate(SLOTS):
            c = along(kind_of(p, m))
            for slot in range(first, first + count):
                odd = slot % 2
                mine = mine_of(c, odd)
                if step == 0:
                    mine = 1 - mine
                total = first_own[p, slot, 2 * kept_set(c, odd) + mine].astype(F32) + first_in[p, slot, mine].astype(F32)
                if step == 0:
                    second_own[p, slot, 0] = total.astype(BF)
                    pair_copy(p, m, odd, 1).start()
                else:
                    mid[0:96, :] = total + second_in[p, slot, 0].astype(F32)

                    @pl.when(kind_of(p, m) == 1)
                    def _():
                        mid[0:96, :] = jnp.dot(swap_v[...], mid[...].astype(BF), preferred_element_type=F32)

                    for d in range(4):
                        rows = mid[24 * d : 24 * d + 24, :]
                        block = jnp.concatenate([rows[:, 0:128], rows[:, 128:]], axis=0)
                        blocks[1][p, d, slot] = block.astype(BF)
            if step == 1:
                for copy in piece_hops(p, m, 1):
                    copy.start()

    def finish_next(p, stage):
        step_wait(p, stage + 1).wait_recv()
        for m, (first, count) in enumerate(SLOTS):
            own = along(axis_of(kind_of(p, m), stage))
            for slot in range(first, first + count):
                total = blocks[stage][p, own, slot].astype(F32)
                for d in range(3):
                    total = total + others[stage][p, d, slot].astype(F32)
                if stage == 1:
                    r = jnp.dot(spread_two, total.astype(BF), preferred_element_type=F32).astype(BF)
                    for d in range(4):
                        blocks[2][p, d, slot] = r[16 * d : 16 * d + 16]
                else:
                    for half in range(2):
                        gws[TAP_OF[slot], :, pl.ds(times(2 * p + half, 128), 128)] = total[8 * half : 8 * half + 8]
            if stage == 1:
                for copy in piece_hops(p, m, 2):
                    copy.start()

    def finish(p, step):
        if step < 2:
            finish_first(p, step)
        else:
            finish_next(p, step - 1)

    def finish_bias(stage):
        bias_wait(stage).wait_recv()
        total = bias_blocks[stage][pos[stage]].astype(F32)
        for d in range(3):
            total = total + bias_others[stage][d].astype(F32)
        if stage == 2:
            gws[TAPS, :, 0:128] = total[0:8]
        else:

            def store(d, value):
                bias_blocks[stage + 1][d] = value

            handed_on(total, stage, store)
            for copy in bias_hops(stage + 1):
                copy.start()

    def hidden(t):
        rows = pl.ds(times(t, TILE), TILE)
        return sum(
            lax.dot_general(g5[rows, k * C : (k + 1) * C], w_v[k * C : (k + 1) * C, :], NT, preferred_element_type=F32)
            for k in range(TAPS)
        )

    def input_gradient(t):
        for i in range(TILE // 32):
            row = pl.multiple_of(t * TILE + i * 32, 32)
            r = jnp.concatenate([rin[pl.ds(row, 32), :]] * (C // 128), axis=1)
            normed = xs[pl.ds(row, 32), :] * r
            dn = dh[i * 32 : i * 32 + 32, :] * gain[...]
            mean = jnp.mean(dn * normed, axis=-1, keepdims=True)
            g = cot_e[pl.ds(row + HALO, 32), :].astype(F32) + (dn - normed * mean) * r
            gi[pl.ds(row, 32), :] = g.astype(BF)

    def backward(t):
        input_gradient(jnp.maximum(t - 1, 0))
        dh[...] = hidden(t)

    mine = (dp * 8 + seq) * 6

    def own_weights():
        base = jnp.minimum((mine >> 4) * 16, C - 32)
        pick_row = lax.broadcasted_iota(jnp.int32, (8, 32), 0)
        pick_col = lax.broadcasted_iota(jnp.int32, (8, 32), 1)
        pick = (pick_col == pick_row + (mine - base)).astype(F32).astype(BF)
        for k in range(TAPS):
            rows = w_v[pl.ds(pl.multiple_of(k * C + base, 16), 32), :]
            w_own[k] = jnp.dot(pick, rows, preferred_element_type=F32)

    def before_last():
        input_gradient(ROWS // TILE - 1)
        for copy in (*halos, h_copy):
            copy.wait_send()
        for p in range(GROUPS):
            g_copy(p).wait_send()
        for p in range(GROUPS - 1):
            for step in range(4):
                step_wait(p, step).wait_send()

    def during(s, start, stop, step):
        if stop > start:
            pl.when((s >= start) & (s < stop))(step)

    def turn_of(s, carry):
        during(s, 0, 3, lambda: forward(s))
        during(s, 2, 3, lambda: finish(0, 0))
        during(s, 3, 4, lambda: finish(0, 1))
        during(s, 1, 4, lambda: weights(s - 1))
        during(s, 4, 8, lambda: backward(s - 4))
        during(s, 6, 7, own_weights)
        during(s, 7, 8, before_last)
        for step in range(4):
            now = (s >= 3 + step) & (s < 5 + step)
            if step < 2:
                pl.when(now)(lambda: finish(s - 2 - step, step))
            else:
                pl.when(now | (s == 1 + step))(lambda: finish(jnp.maximum(s - 2 - step, 0), step))
            if step < 3:
                during(s, 5 + step, 6 + step, lambda: finish_bias(step))
        return carry

    norm()
    turn()
    norm_ends()
    shift_h()
    dh[...] = jnp.zeros(dh.shape, F32)
    lax.fori_loop(0, 8, turn_of, 0)

    gw[...] = gws[0:TAPS, 0:6, :]
    total = jnp.zeros((8, C), F32)
    for k in range(TAPS):
        total = total + w_own[k] * gws[k]
    lane = lax.broadcasted_iota(jnp.int32, (8, C), 1)
    row = lax.broadcasted_iota(jnp.int32, (8, C), 0)
    own_gain = jnp.sum(jnp.where(lane == row + mine, gain[...], 0.0), axis=-1, keepdims=True)
    column = jnp.sum(total, axis=-1, keepdims=True) / own_gain
    diagonal = (lane == row)[:, 0:128] & (row < 6)[:, 0:128]
    small[0:1, :] = jnp.sum(jnp.where(diagonal, gws[TAPS, :, 0:128], 0.0), axis=0, keepdims=True)
    small[1:2, :] = jnp.sum(jnp.where(diagonal, column, 0.0), axis=0, keepdims=True)

    for stage in range(STAGES):
        bias_wait(stage).wait_send()
    for step in range(4):
        step_wait(GROUPS - 1, step).wait_send()


MESH = pl.DeviceIdType.MESH


def body(bases, upsampled, base_table, filter_weight, filter_bias, norm_gain, cotangent):
    vmem, hbm = pl.BlockSpec(memory_space=pltpu.VMEM), pl.BlockSpec(memory_space=pl.ANY)
    scratch = [
        pltpu.VMEM((1, ROWS + 256), jnp.int32),
        pltpu.VMEM((EXT, C), BF),
        pltpu.VMEM((EXT, C), BF),
        pltpu.VMEM((TAPS * C, C), BF),
        pltpu.VMEM((C, C), BF),
        pltpu.VMEM((HALF, HALF), BF),
        pltpu.VMEM((8, C), F32),
        pltpu.VMEM((ROWS, C), F32),
        pltpu.VMEM((ROWS, 128), F32),
        pltpu.VMEM((EXT + 2 * HALO, C), BF),
        pltpu.VMEM((EXT, TAPS * C), BF),
        pltpu.VMEM((2, HALF, ROWS), BF),
        pltpu.VMEM((HALF, ROWS), BF),
        pltpu.VMEM((EXT, WIDE), F32),
        pltpu.VMEM((GROUPS, EXT, WIDE), BF),
        pltpu.VMEM((GROUPS, EXT, WIDE), BF),
        pltpu.VMEM((ROWS, TAPS * C), BF),
        pltpu.VMEM((ROWS, TAPS * WIDE), BF),
        pltpu.VMEM((8, C), F32),
        pltpu.VMEM((TILE, C), F32),
        pltpu.VMEM((TAPS + 1, 8, C), F32),
        pltpu.VMEM((1, C), F32),
        pltpu.VMEM((1, C), F32),
    ]
    scratch += [pltpu.VMEM((GROUPS, TAPS, n, 96, WIDE), BF) for n in (4, 2, 1, 1)]
    scratch += [pltpu.VMEM((GROUPS, 4, TAPS, rows, 128), BF) for rows in (48, 16)]
    scratch += [pltpu.VMEM((GROUPS, 3, TAPS, rows, 128), BF) for rows in (48, 16)]
    scratch += [pltpu.VMEM((4, rows, 128), BF) for rows in BLOCK_ROWS]
    scratch += [pltpu.VMEM((3, rows, 128), BF) for rows in BLOCK_ROWS]
    scratch += [pltpu.VMEM((HALF, 2 * WIDE), F32), pltpu.VMEM((128, WIDE), F32), pltpu.VMEM((96, 128), BF)]
    scratch += [pltpu.VMEM((TAPS, 8, C), F32)]
    remotes = 10 + 4 * GROUPS + STAGES
    scratch += [
        pltpu.SemaphoreType.DMA((16,)),
        pltpu.SemaphoreType.DMA((remotes,)),
        pltpu.SemaphoreType.DMA((remotes,)),
    ]
    out, gin, gw, small = pl.pallas_call(
        kernel,
        out_shape=[
            pltpu.VMEM((ROWS, C), BF),
            pltpu.VMEM((ROWS, C), BF),
            pltpu.VMEM((TAPS, 6, C), F32),
            pltpu.VMEM((8, 128), F32),
        ],
        in_specs=[hbm, hbm, vmem, hbm, hbm, hbm, hbm],
        out_specs=[vmem, vmem, vmem, vmem],
        scratch_shapes=scratch,
        compiler_params=pltpu.CompilerParams(collective_id=0, has_side_effects=True, vmem_limit_bytes=58 * 2**20),
        name="block",
    )(
        bases,
        upsampled[0],
        base_table,
        filter_weight.reshape(TAPS * C, C),
        filter_bias,
        norm_gain,
        cotangent[0],
    )
    return out[None], gin[None], gw, small[0, 0:6], small[1, 0:6]


def solution(mesh):
    placed = (P("dp", "seq"), P("dp", "seq", None), P(), P(), P(), P(), P("dp", "seq", None))
    return jax.shard_map(
        body,
        mesh=mesh,
        in_specs=placed,
        out_specs=(
            P("dp", "seq", None),
            P("dp", "seq", None),
            P(None, ("dp", "seq"), None),
            P(("dp", "seq")),
            P(("dp", "seq")),
        ),
        check_vma=False,
    )
```
